32 devices in a mesh: dom: 16 (over z, y, x), feat: 2 (over core).
Axes of the slice: x: 2, y: 2, z: 4, core: 2. Of those that a mesh axis runs over, the one named last changes fastest.
Arguments:
- features: bfloat16 [65536, 256], P('dom', 'feat'), may hold values from -6 to 6
- self_weight: bfloat16 [256, 256], P('feat'), may hold values from -0.375 to 0.375
- neighbor_weight: bfloat16 [256, 256], P('feat'), may hold values from -0.375 to 0.375
- tile_values: bfloat16 [2560, 128, 128], P('dom'), may hold values from 0 to 1
- tile_row: int32 [2560], P('dom'), may hold values from 0 to 31
- tile_owner: int32 [2560], P('dom'), may hold values from 0 to 15
- send_tile: int32 [256], P('dom'), may hold values from 0 to 31
- tile_count: int32 [16], P('dom'), may hold values from 26 to 160, as said below
- hub_panel: bfloat16 [65536, 32], P('dom'), may hold values from 0 to 1
- hub_rows: int32 [32], P('dom'), may hold values from 0 to 4095
- cotangent: bfloat16 [65536, 256], P('dom', 'feat'), may hold values from -6 to 6
Outputs:
- layer_out: bfloat16 [65536, 256], P('dom', 'feat')
- self_grad: float32 [256, 256], P('feat')
- neighbor_grad: float32 [256, 256], P('feat')
- input_grad: float32 [65536, 256], P('dom', 'feat')
The draws below stay inside these ranges and needn't reach their ends.
Inputs may be any that keep to these rules, and one draw needn't show every extreme that they name: `tile_count`: one partition has exactly 160 live slots in every draw.
All inputs are finite; a program needn't handle non-finite values.
Results may differ from the reference program's by a relative error of at most 0.011.
The reference program's roundings to bfloat16 on the way count: a program that leaves them out, or rounds other values in their place, can miss the bound.
Values may be sent and summed in bfloat16 or wider, within the bound.
A program may use at most 128 MiB of HBM per device.

```python
import math
import jax
import jax.numpy as jnp
from jax import lax

D = 256
TILE = 128
HUB_DEV = 2
V_DEV = 4096
TILES_DEV = 32
TILE_CAP = 160
HUBS = 32
V = 65536
N_DOM = 16


def draw_tile_owner(key, part):
    keys = jax.random.split(key, N_DOM)
    orders = jax.vmap(lambda single: jax.random.permutation(single, N_DOM))(keys)
    picks = jnp.arange(TILE_CAP) % N_DOM
    return orders[:, picks].reshape(N_DOM * TILE_CAP).astype(jnp.int32)


def draw_tile_count(key, part):
    counts = jax.random.randint(key, (N_DOM,), TILE_CAP // 6, TILE_CAP // 2 + 1)
    chosen = jax.random.randint(jax.random.fold_in(key, 7), (), 0, N_DOM)
    return jnp.where(jnp.arange(N_DOM) == chosen, TILE_CAP, counts).astype(jnp.int32)


def set_ends(result, stream_key, smallest, top_value):
    spot = [jax.random.randint(jax.random.fold_in(stream_key, axis), (), 0, length) for axis, length in enumerate(result.shape)]
    widest = result.shape.index(max(result.shape))
    next_to = spot[:widest] + [(spot[widest] + 1) % result.shape[widest]] + spot[widest + 1:]
    return result.at[tuple(spot)].set(smallest).at[tuple(next_to)].set(top_value)


def block_scale(rng, shape, shards, smallest, largest):
    loudness, own = 1.0, jax.random.fold_in(rng, 6)
    for dim, parts in shards:
        draws = jnp.exp(jax.random.uniform(jax.random.fold_in(own, dim), (parts,), jnp.float32, smallest / len(shards), largest / len(shards)))
        loudness = loudness * jnp.repeat(draws, shape[dim] // parts).reshape([-1 if axis == dim else 1 for axis in range(len(shape))])
    return loudness


def normal_values(key, dims, spread, reach, shards=(), kind=jnp.bfloat16):
    array = spread * jax.random.normal(key, dims, jnp.float32)
    if shards:
        array = array * block_scale(key, dims, shards, -0.22, 0.18)
    return jnp.clip(array, -reach, reach).astype(kind)


def setup_inputs(seed: int = 0) -> dict:
    seeds = jax.random.split(jax.random.key(seed), 12)
    features = normal_values(seeds[0], (V, D), 1.0, 6.0, ((0, 16), (1, 2)))
    self_weight = normal_values(seeds[1], (D, D), D ** -0.5, 0.375, ((0, 2),))
    neighbor_weight = normal_values(seeds[2], (D, D), D ** -0.5, 0.375, ((0, 2),))
    tile_values = jnp.clip(1.0 * jax.random.uniform(seeds[3], (N_DOM * TILE_CAP, TILE, TILE), jnp.float32) ** block_scale(seeds[3], (N_DOM * TILE_CAP, TILE, TILE), ((0, 16),), -0.2, 0.2), 0.0, 1.0).astype(jnp.bfloat16)
    tile_row = set_ends(jax.random.randint(seeds[4], (N_DOM * TILE_CAP,), 0, TILES_DEV), jax.random.fold_in(seeds[4], 1), 0, TILES_DEV - 1).astype(jnp.int32)
    tile_owner = draw_tile_owner(jax.random.fold_in(seeds[11], 71), 0)
    send_tile = set_ends(jax.random.randint(seeds[6], (N_DOM * N_DOM,), 0, TILES_DEV), jax.random.fold_in(seeds[6], 1), 0, TILES_DEV - 1).astype(jnp.int32)
    tile_count = draw_tile_count(jax.random.fold_in(seeds[11], 71), 0)
    hub_panel = jnp.clip(1.0 * jax.random.uniform(seeds[8], (V, HUBS), jnp.float32) ** block_scale(seeds[8], (V, HUBS), ((0, 16),), -0.2, 0.2), 0.0, 1.0).astype(jnp.bfloat16)
    hub_rows = set_ends(jax.random.randint(seeds[9], (HUBS,), 0, V_DEV), jax.random.fold_in(seeds[9], 1), 0, V_DEV - 1).astype(jnp.int32)
    cotangent = normal_values(seeds[10], (V, D), 1.0, 6.0, ((0, 16), (1, 2)))
    return {"features": features, "self_weight": self_weight, "neighbor_weight": neighbor_weight, "tile_values": tile_values, "tile_row": tile_row, "tile_owner": tile_owner, "send_tile": send_tile, "tile_count": tile_count, "hub_panel": hub_panel, "hub_rows": hub_rows, "cotangent": cotangent}


def reference(features, self_weight, neighbor_weight, tile_values, tile_row, tile_owner, send_tile, tile_count, hub_panel, hub_rows, cotangent):
    tiles_dev = V_DEV // TILE
    highest = lax.Precision.HIGHEST
    feature_tiles = features.reshape(N_DOM, tiles_dev, TILE, D)
    values_all = tile_values.reshape(N_DOM, TILE_CAP, TILE, TILE)
    rows_all = tile_row.reshape(N_DOM, TILE_CAP)
    owners_all = tile_owner.reshape(N_DOM, TILE_CAP)
    sends = send_tile.reshape(N_DOM, N_DOM)
    panels = hub_panel.reshape(N_DOM, V_DEV, HUBS)
    local_feats = features.reshape(N_DOM, V_DEV, D)
    local_cot = cotangent.reshape(N_DOM, V_DEV, D)
    hub_owner = (jnp.arange(HUBS) // HUB_DEV).astype(jnp.int32)
    hub_global = (hub_owner * V_DEV + hub_rows).astype(jnp.int32)
    hub_feats = features[hub_global].astype(jnp.float32)
    every_owner = jnp.arange(N_DOM).astype(jnp.int32)

    def step(carry, index):
        remote, hub_acc, self_acc, neigh_acc = carry
        values = values_all[index].astype(jnp.float32)
        rows = rows_all[index]
        owners = owners_all[index]
        live = (jnp.arange(TILE_CAP) < tile_count[index]).astype(jnp.float32)
        col_tiles = sends[owners, index]
        columns = feature_tiles[owners, col_tiles].astype(jnp.float32)
        products = jnp.einsum('kij,kjf->kif', values, columns, precision=highest) * live[:, None, None]
        panel = panels[index].astype(jnp.float32)
        sums = jax.ops.segment_sum(products, rows, num_segments=tiles_dev).reshape(V_DEV, D)
        sums = sums + jnp.dot(panel, hub_feats, precision=highest)
        tile_squares = lax.optimization_barrier(jnp.sum(values * values, axis=2)) * live[:, None]
        squares = jax.ops.segment_sum(tile_squares, rows, num_segments=tiles_dev).reshape(V_DEV)
        squares = squares + lax.optimization_barrier(jnp.sum(panel * panel, axis=1))
        inverse_norm = lax.rsqrt(1.0 + squares)
        aggregate = (sums * inverse_norm[:, None]).astype(jnp.bfloat16)
        x_here = local_feats[index]
        preact = jnp.dot(x_here, self_weight, preferred_element_type=jnp.float32) + jnp.dot(aggregate, neighbor_weight, preferred_element_type=jnp.float32)
        layer_part = jnp.maximum(preact, 0.0).astype(jnp.bfloat16)
        slopes = jnp.where(preact > 0, local_cot[index].astype(jnp.float32), 0.0).astype(jnp.bfloat16)
        self_acc = self_acc + jnp.dot(x_here.T, slopes, preferred_element_type=jnp.float32)
        neigh_acc = neigh_acc + jnp.dot(aggregate.T, slopes, preferred_element_type=jnp.float32)
        direct = jnp.dot(slopes, self_weight.T, preferred_element_type=jnp.float32)
        agg_slopes = (jnp.dot(slopes, neighbor_weight.T, preferred_element_type=jnp.float32) * inverse_norm[:, None]).astype(jnp.bfloat16)
        slope_tiles = agg_slopes.reshape(tiles_dev, TILE, D)[rows].astype(jnp.float32)
        tile_back = jnp.einsum('kji,kjf->kif', values, slope_tiles, precision=highest) * live[:, None, None]
        owner_terms = jax.ops.segment_sum(tile_back, owners, num_segments=N_DOM).astype(jnp.bfloat16).astype(jnp.float32)
        remote = remote.at[every_owner, sends[:, index]].add(owner_terms)
        hub_acc = hub_acc + jnp.dot(panel.T, agg_slopes.astype(jnp.float32), precision=highest)
        return ((remote, hub_acc, self_acc, neigh_acc), (layer_part, direct))
    start = (jnp.zeros((N_DOM, tiles_dev, TILE, D), jnp.float32), jnp.zeros((HUBS, D), jnp.float32), jnp.zeros((D, D), jnp.float32), jnp.zeros((D, D), jnp.float32))
    final, stacked = lax.scan(step, start, jnp.arange(N_DOM, dtype=jnp.int32))
    remote, hub_acc, self_acc, neigh_acc = final
    layer_parts, directs = stacked
    factor = 1.0 / math.sqrt(N_DOM * V_DEV)
    input_grad = directs.reshape(N_DOM * V_DEV, D) + remote.reshape(N_DOM * V_DEV, D)
    input_grad = input_grad.at[hub_global].add(hub_acc)
    return (layer_parts.reshape(N_DOM * V_DEV, D), self_acc * factor, neigh_acc * factor, input_grad)
```

```python
import functools
import math

import jax
import jax.numpy as jnp
from jax import lax
from jax.experimental import pallas as pl
from jax.experimental.pallas import tpu as pltpu
from jax.sharding import PartitionSpec as P

F32 = jnp.float32
BF16 = jnp.bfloat16
VMEM_BYTES = 58 * 2**20
UNROLL = 4


def vmem():
    return pl.BlockSpec(memory_space=pltpu.VMEM)


def smem():
    return pl.BlockSpec(memory_space=pltpu.SMEM)


def dot(a, b, dims=((1,), (0,))):
    return lax.dot_general(a, b, (dims, ((), ())), preferred_element_type=F32)


def greet(n, me, feat, with_sibling):
    barrier = pltpu.get_barrier_semaphore()

    def hello(d, carry):
        pl.semaphore_signal(
            barrier, inc=1, device_id={"dom": lax.rem(me + d, n)}, device_id_type=pl.DeviceIdType.MESH
        )
        return carry

    lax.fori_loop(1, n, hello, 0)
    if with_sibling:
        pl.semaphore_signal(barrier, inc=1, device_id={"feat": 1 - feat}, device_id_type=pl.DeviceIdType.MESH)
    pl.semaphore_wait(barrier, n if with_sibling else n - 1)


def exchange_kernel(
    n, hub_dev, feat_ref, cot_ref, ws_ref, wn_ref, send_ref, hub_ref,
    cols_ref, x_ref, c_ref, wso_ref, wno_ref,
    stage, send_sem, recv_sem, fsend_sem, frecv_sem, loc_sem, esend_sem, erecv_sem,
):
    me = lax.axis_index("dom")
    feat = lax.axis_index("feat")
    edge = feat_ref.shape[1]
    rows = edge * feat_ref.shape[0]
    pad = stage.shape[1] - edge
    half = feat_ref.shape[2]
    greet(n, me, feat, True)

    row_ids = lax.broadcasted_iota(jnp.int32, (edge, half), 0)
    out_ids = lax.broadcasted_iota(jnp.int32, (pad, half), 0)
    hub_block = jnp.zeros((pad, half), F32)
    for h in range(hub_dev):
        r = hub_ref[h]
        tile = feat_ref[r // edge].astype(F32)
        row = jnp.sum(jnp.where(row_ids == r % edge, tile, 0.0), axis=0, keepdims=True)
        hub_block = jnp.where(out_ids == h, row, hub_block)
    hub_block = hub_block.astype(BF16)

    def peer_copy(d):
        return pltpu.make_async_remote_copy(
            src_ref=stage.at[d], dst_ref=cols_ref.at[me, :, 0:half],
            send_sem=send_sem.at[d], recv_sem=recv_sem.at[d],
            device_id={"dom": lax.rem(me + d, n)}, device_id_type=pl.DeviceIdType.MESH,
        )

    def forward(q):
        return pltpu.make_async_remote_copy(
            src_ref=cols_ref.at[q, :, 0:half], dst_ref=cols_ref.at[q, :, half:2 * half],
            send_sem=fsend_sem.at[q], recv_sem=frecv_sem.at[q],
            device_id={"feat": 1 - feat}, device_id_type=pl.DeviceIdType.MESH,
        )

    def send(d, carry):
        q = lax.rem(me + d, n)
        stage[d, 0:edge, :] = feat_ref[send_ref[q]]
        stage[d, edge:, :] = hub_block
        peer_copy(d).start()
        return carry

    lax.fori_loop(1, n, send, 0)
    cols_ref[me, 0:edge, 0:half] = feat_ref[send_ref[me]]
    cols_ref[me, edge:, 0:half] = hub_block
    forward(me).start()

    extras = [
        pltpu.make_async_remote_copy(
            src_ref=src, dst_ref=dst, send_sem=esend_sem.at[i], recv_sem=erecv_sem.at[i],
            device_id={"feat": 1 - feat}, device_id_type=pl.DeviceIdType.MESH,
        )
        for i, (src, dst) in enumerate((
            (feat_ref, x_ref.at[:, :, half:2 * half]),
            (cot_ref, c_ref.at[:, :, half:2 * half]),
            (ws_ref, wso_ref),
            (wn_ref, wno_ref),
        ))
    ]
    for copy in extras:
        copy.start()
    locals_ = [
        pltpu.make_async_copy(feat_ref, x_ref.at[:, :, 0:half], loc_sem.at[0]),
        pltpu.make_async_copy(cot_ref, c_ref.at[:, :, 0:half], loc_sem.at[1]),
    ]
    for copy in locals_:
        copy.start()

    def arrive(d, carry):
        peer_copy(d).wait_recv()
        forward(lax.rem(me - d + n, n)).start()
        return carry

    lax.fori_loop(1, n, arrive, 0)
    for copy in locals_:
        copy.wait()
    for copy in extras:
        copy.wait()

    def finish(d, carry):
        peer_copy(d).wait_send()
        return carry

    lax.fori_loop(1, n, finish, 0)

    def finish_forward(q, carry):
        forward(q).wait()
        return carry

    lax.fori_loop(0, n, finish_forward, 0)


def slot_loop(count, step):
    full = count // UNROLL

    def many(i, carry):
        for u in range(UNROLL):
            step(i * UNROLL + u)
        return carry

    lax.fori_loop(0, full, many, 0)

    def single(k, carry):
        step(k)
        return carry

    lax.fori_loop(full * UNROLL, count, single, 0)


def local_kernel(
    hub_dev, feat_ref, row_ref, owner_ref, count_ref,
    cols_ref, x_ref, c_ref, ws_ref, wn_ref, wso_ref, wno_ref, val_ref, panel_ref,
    out_ref, grad_ref, direct_ref, terms_ref,
    acc, sq, slopes_t, terms_t, hub_s,
):
    f = feat_ref[0]
    tiles, edge, wide = x_ref.shape
    half = wide // 2
    n = cols_ref.shape[0]
    hubs = panel_ref.shape[2]
    pad = cols_ref.shape[1] - edge
    count = count_ref[0]

    def local_order(w):
        return jnp.where(f == 0, w, jnp.concatenate([w[:, half:], w[:, :half]], axis=1))

    ws_own = local_order(ws_ref[...].astype(F32)).astype(BF16)
    wn_own = local_order(wn_ref[...].astype(F32)).astype(BF16)
    ws_all = jnp.concatenate([ws_own, local_order(wso_ref[...].astype(F32)).astype(BF16)], axis=0)
    wn_all = jnp.concatenate([wn_own, local_order(wno_ref[...].astype(F32)).astype(BF16)], axis=0)

    hub_ids = lax.broadcasted_iota(jnp.int32, (hubs, n * pad), 0)
    place = lax.broadcasted_iota(jnp.int32, (hubs, n * pad), 1)
    pick = (hub_ids // hub_dev == place // pad) & (hub_ids % hub_dev == place % pad)
    hub_rows = cols_ref[:, edge:, :].reshape(n * pad, wide)
    hub_feats = dot(jnp.where(pick, 1.0, 0.0).astype(BF16), hub_rows).astype(BF16)

    def start(t, carry):
        panel = panel_ref[t]
        acc[t] = dot(panel, hub_feats)
        sq[t] = jnp.zeros((edge, edge), F32)
        return carry

    lax.fori_loop(0, tiles, start, 0)

    def ahead(k):
        values = val_ref[k]
        row = row_ref[k]
        acc[row] += dot(values, cols_ref[owner_ref[k], 0:edge, :])
        wide_values = values.astype(F32)
        sq[row] += wide_values * wide_values

    slot_loop(count, ahead)

    grad_ref[...] = jnp.zeros_like(grad_ref)
    hub_s[...] = jnp.zeros_like(hub_s)

    def dense(t, carry):
        panel = panel_ref[t]
        wide_panel = panel.astype(F32)
        squares = jnp.sum(sq[t], axis=1, keepdims=True) + jnp.sum(wide_panel * wide_panel, axis=1, keepdims=True)
        inverse = lax.rsqrt(1.0 + squares)
        aggregate = (acc[t] * inverse).astype(BF16)
        x = x_ref[t]
        preact = dot(x, ws_all) + dot(aggregate, wn_all)
        out_ref[t] = jnp.maximum(preact[:, :half], 0.0).astype(BF16)
        slopes = jnp.where(preact > 0, c_ref[t].astype(F32), 0.0).astype(BF16)
        direct_ref[t] = dot(slopes, ws_own, ((1,), (1,)))
        back = dot(slopes, wn_own, ((1,), (1,))) * inverse
        back_t = back.T.astype(BF16)
        slopes_t[t] = back_t
        hub_s[...] += dot(back_t, panel)
        left = jnp.concatenate([x[:, :half], aggregate[:, :half]], axis=1)
        grad_ref[...] += dot(left, slopes, ((0,), (0,)))
        return carry

    lax.fori_loop(0, tiles, dense, 0)

    def clear(o, carry):
        terms_t[o] = jnp.zeros((half, edge), F32)
        return carry

    lax.fori_loop(0, n, clear, 0)

    def behind(k):
        terms_t[owner_ref[k]] += dot(slopes_t[row_ref[k]], val_ref[k])

    slot_loop(count, behind)

    hub_terms = hub_s[...].T
    high = hub_terms.astype(BF16)
    low = (hub_terms - high.astype(F32)).astype(BF16)
    ids = lax.broadcasted_iota(jnp.int32, (n * pad, hubs), 1)
    spot = lax.broadcasted_iota(jnp.int32, (n * pad, hubs), 0)
    same = ids // hub_dev == spot // pad
    put_high = jnp.where(same & (spot % pad == ids % hub_dev), 1.0, 0.0).astype(BF16)
    put_low = jnp.where(same & (spot % pad == ids % hub_dev + hub_dev), 1.0, 0.0).astype(BF16)
    blocks = dot(put_high, high) + dot(put_low, low)
    terms_ref[:, edge:, :] = blocks.reshape(n, pad, half).astype(BF16)

    def emit(o, carry):
        terms_ref[o, 0:edge, :] = terms_t[o].T.astype(BF16)
        return carry

    lax.fori_loop(0, n, emit, 0)


def return_kernel(n, reduce_here, factor, *refs):
    if reduce_here:
        (terms_ref, grad_ref, back_ref, self_ref, neigh_ref,
         send_sem, recv_sem, gstage, gin, gall, rsend, rrecv, asend, arecv) = refs
    else:
        terms_ref, back_ref, send_sem, recv_sem = refs
    me = lax.axis_index("dom")
    feat = lax.axis_index("feat")
    greet(n, me, feat, False)

    def copy_to(d, src, dst, ssem, rsem):
        return pltpu.make_async_remote_copy(
            src_ref=src, dst_ref=dst, send_sem=ssem.at[d], recv_sem=rsem.at[d],
            device_id={"dom": lax.rem(me + d, n)}, device_id_type=pl.DeviceIdType.MESH,
        )

    def term_copy(d):
        return copy_to(d, terms_ref.at[lax.rem(me + d, n)], back_ref.at[me], send_sem, recv_sem)

    def each(fn):
        def body(d, carry):
            fn(d)
            return carry
        lax.fori_loop(1, n, body, 0)

    if reduce_here:
        piece = grad_ref.shape[0] // n

        def part_copy(d):
            return copy_to(d, gstage.at[lax.rem(me + d, n)], gin.at[me], rsend, rrecv)

        def all_copy(d):
            return copy_to(d, gall.at[me], gall.at[me], asend, arecv)

        gstage[...] = grad_ref[...].astype(BF16).reshape(gstage.shape)
        each(lambda d: part_copy(d).start())
    each(lambda d: term_copy(d).start())
    back_ref[me] = terms_ref[me]
    if reduce_here:
        gin[me] = gstage[me]
        each(lambda d: part_copy(d).wait_recv())
        gall[me] = jnp.sum(gin[...].astype(F32), axis=0).astype(BF16)
        each(lambda d: all_copy(d).start())
    each(lambda d: term_copy(d).wait())
    if reduce_here:
        each(lambda d: part_copy(d).wait_send())
        each(lambda d: all_copy(d).wait())
        total = gall[...].astype(F32).reshape(grad_ref.shape) * factor
        half = total.shape[1] // 2
        total = jnp.where(feat == 0, total, jnp.concatenate([total[:, half:], total[:, :half]], axis=1))
        self_ref[...] = total[: self_ref.shape[0]]
        neigh_ref[...] = total[self_ref.shape[0]:]


def finish_kernel(hub_dev, send_ref, hub_ref, direct_ref, back_ref, out_ref):
    n = back_ref.shape[0]
    edge = 128
    out_ref[...] = direct_ref[...]

    def add(q, carry):
        rows = pl.ds(pl.multiple_of(send_ref[q] * edge, edge), edge)
        out_ref[rows, :] += back_ref[q, 0:edge, :].astype(F32)
        return carry

    lax.fori_loop(0, n, add, 0)

    def gather(q, total):
        return total + back_ref[q, edge:, :].astype(F32)

    total = lax.fori_loop(0, n, gather, jnp.zeros((back_ref.shape[1] - edge, back_ref.shape[2]), F32))
    for h in range(hub_dev):
        row = total[h:h + 1] + total[hub_dev + h:hub_dev + h + 1]
        out_ref[pl.ds(hub_ref[h], 1), :] += row


def shards(
    features, self_weight, neighbor_weight, tile_values, tile_row, tile_owner,
    send_tile, tile_count, hub_panel, hub_rows, cotangent,
):
    rows, half = features.shape
    edge = tile_values.shape[1]
    tiles = rows // edge
    n = lax.axis_size("dom")
    hub_dev = hub_rows.shape[0]
    hubs = hub_panel.shape[1]
    wide = 2 * half
    pad = -(-2 * hub_dev // 16) * 16
    tall = edge + pad
    sds = jax.ShapeDtypeStruct
    dma = pltpu.SemaphoreType.DMA
    params = functools.partial(pltpu.CompilerParams, vmem_limit_bytes=VMEM_BYTES)

    cols, x_all, c_all, ws_other, wn_other = pl.pallas_call(
        functools.partial(exchange_kernel, n, hub_dev),
        out_shape=(
            sds((n, tall, wide), BF16), sds((tiles, edge, wide), BF16), sds((tiles, edge, wide), BF16),
            sds(self_weight.shape, BF16), sds(neighbor_weight.shape, BF16),
        ),
        in_specs=[vmem()] * 4 + [smem()] * 2,
        out_specs=(vmem(),) * 5,
        scratch_shapes=[
            pltpu.VMEM((n, tall, half), BF16),
            dma((n,)), dma((n,)), dma((n,)), dma((n,)), dma((2,)), dma((4,)), dma((4,)),
        ],
        compiler_params=params(collective_id=0, has_side_effects=True),
        name="exchange",
    )(
        features.reshape(tiles, edge, half), cotangent.reshape(tiles, edge, half),
        self_weight, neighbor_weight, send_tile, hub_rows,
    )

    feat_index = lax.axis_index("feat").astype(jnp.int32).reshape(1)
    layer, grads, direct, terms = pl.pallas_call(
        functools.partial(local_kernel, hub_dev),
        out_shape=(
            sds((tiles, edge, half), BF16), sds((wide, wide), F32),
            sds((tiles, edge, half), F32), sds((n, tall, half), BF16),
        ),
        in_specs=[smem()] * 4 + [vmem()] * 9,
        out_specs=(vmem(),) * 4,
        scratch_shapes=[
            pltpu.VMEM((tiles, edge, wide), F32),
            pltpu.VMEM((tiles, edge, edge), F32),
            pltpu.VMEM((tiles, half, edge), BF16),
            pltpu.VMEM((n, half, edge), F32),
            pltpu.VMEM((half, hubs), F32),
        ],
        compiler_params=params(),
        name="local_pass",
    )(
        feat_index, tile_row, tile_owner, tile_count, cols, x_all, c_all,
        self_weight, neighbor_weight, ws_other, wn_other, tile_values,
        hub_panel.reshape(tiles, edge, hubs),
    )

    factor = 1.0 / math.sqrt(rows * n)
    reduce_here = wide % (16 * n) == 0
    back_shape = sds((n, tall, half), BF16)
    if reduce_here:
        part = (n, wide // n, wide)
        back, self_grad, neighbor_grad = pl.pallas_call(
            functools.partial(return_kernel, n, True, factor),
            out_shape=(back_shape, sds((half, wide), F32), sds((half, wide), F32)),
            in_specs=[vmem()] * 2,
            out_specs=(vmem(),) * 3,
            scratch_shapes=[dma((n,)), dma((n,))] + [pltpu.VMEM(part, BF16)] * 3 + [dma((n,))] * 4,
            compiler_params=params(collective_id=1, has_side_effects=True),
            name="send_back",
        )(terms, grads)
    else:
        back = pl.pallas_call(
            functools.partial(return_kernel, n, False, factor),
            out_shape=back_shape,
            in_specs=[vmem()],
            out_specs=vmem(),
            scratch_shapes=[dma((n,)), dma((n,))],
            compiler_params=params(collective_id=1, has_side_effects=True),
            name="send_back",
        )(terms)
        total = lax.psum(grads, "dom") * factor
        swapped = jnp.concatenate([total[:, half:], total[:, :half]], axis=1)
        total = jnp.where(feat_index[0] == 0, total, swapped)
        self_grad, neighbor_grad = total[:half], total[half:]

    input_grad = pl.pallas_call(
        functools.partial(finish_kernel, hub_dev),
        out_shape=sds((rows, half), F32),
        in_specs=[smem()] * 2 + [vmem()] * 2,
        out_specs=vmem(),
        compiler_params=params(),
        name="finish",
    )(send_tile, hub_rows, direct.reshape(rows, half), back)
    return layer.reshape(rows, half), self_grad, neighbor_grad, input_grad


def solution(mesh):
    placed = (
        P("dom", "feat"), P("feat", None), P("feat", None), P("dom", None, None), P("dom"), P("dom"),
        P("dom"), P("dom"), P("dom", None), P("dom"), P("dom", "feat"),
    )
    return jax.shard_map(
        shards,
        mesh=mesh,
        in_specs=placed,
        out_specs=(P("dom", "feat"), P("feat", None), P("feat", None), P("dom", "feat")),
        check_vma=False,
    )
```

```python
import functools
import math

import jax
import jax.numpy as jnp
from jax import lax
from jax.experimental import pallas as pl
from jax.experimental.pallas import tpu as pltpu
from jax.sharding import PartitionSpec as P

F32 = jnp.float32
BF16 = jnp.bfloat16
VMEM_BYTES = 58 * 2**20
UNROLL = 8


def vmem():
    return pl.BlockSpec(memory_space=pltpu.VMEM)


def smem():
    return pl.BlockSpec(memory_space=pltpu.SMEM)


def dot(a, b, dims=((1,), (0,))):
    return lax.dot_general(a, b, (dims, ((), ())), preferred_element_type=F32)


def greet(n, me, feat, with_sibling):
    barrier = pltpu.get_barrier_semaphore()

    def hello(d, carry):
        pl.semaphore_signal(
            barrier, inc=1, device_id={"dom": lax.rem(me + d, n)}, device_id_type=pl.DeviceIdType.MESH
        )
        return carry

    lax.fori_loop(1, n, hello, 0)
    if with_sibling:
        pl.semaphore_signal(barrier, inc=1, device_id={"feat": 1 - feat}, device_id_type=pl.DeviceIdType.MESH)
    pl.semaphore_wait(barrier, n if with_sibling else n - 1)


def exchange_kernel(
    n, hub_dev, feat_ref, cot_ref, ws_ref, wn_ref, send_ref, hub_ref,
    cols_ref, x_ref, c_ref, wso_ref, wno_ref,
    stage, send_sem, recv_sem, fsend_sem, frecv_sem, loc_sem, esend_sem, erecv_sem,
):
    me = lax.axis_index("dom")
    feat = lax.axis_index("feat")
    edge = feat_ref.shape[1]
    rows = edge * feat_ref.shape[0]
    pad = stage.shape[1] - edge
    half = feat_ref.shape[2]
    greet(n, me, feat, True)

    row_ids = lax.broadcasted_iota(jnp.int32, (edge, half), 0)
    out_ids = lax.broadcasted_iota(jnp.int32, (pad, half), 0)
    hub_block = jnp.zeros((pad, half), F32)
    for h in range(hub_dev):
        r = hub_ref[h]
        tile = feat_ref[r // edge].astype(F32)
        row = jnp.sum(jnp.where(row_ids == r % edge, tile, 0.0), axis=0, keepdims=True)
        hub_block = jnp.where(out_ids == h, row, hub_block)
    hub_block = hub_block.astype(BF16)

    def peer_copy(d):
        return pltpu.make_async_remote_copy(
            src_ref=stage.at[d], dst_ref=cols_ref.at[me, :, 0:half],
            send_sem=send_sem.at[d], recv_sem=recv_sem.at[d],
            device_id={"dom": lax.rem(me + d, n)}, device_id_type=pl.DeviceIdType.MESH,
        )

    def forward(q):
        return pltpu.make_async_remote_copy(
            src_ref=cols_ref.at[q, :, 0:half], dst_ref=cols_ref.at[q, :, half:2 * half],
            send_sem=fsend_sem.at[q], recv_sem=frecv_sem.at[q],
            device_id={"feat": 1 - feat}, device_id_type=pl.DeviceIdType.MESH,
        )

    def send(d, carry):
        q = lax.rem(me + d, n)
        stage[d, 0:edge, :] = feat_ref[send_ref[q]]
        stage[d, edge:, :] = hub_block
        peer_copy(d).start()
        return carry

    lax.fori_loop(1, n, send, 0)
    cols_ref[me, 0:edge, 0:half] = feat_ref[send_ref[me]]
    cols_ref[me, edge:, 0:half] = hub_block
    forward(me).start()

    extras = [
        pltpu.make_async_remote_copy(
            src_ref=src, dst_ref=dst, send_sem=esend_sem.at[i], recv_sem=erecv_sem.at[i],
            device_id={"feat": 1 - feat}, device_id_type=pl.DeviceIdType.MESH,
        )
        for i, (src, dst) in enumerate((
            (feat_ref, x_ref.at[:, :, half:2 * half]),
            (cot_ref, c_ref.at[:, :, half:2 * half]),
            (ws_ref, wso_ref),
            (wn_ref, wno_ref),
        ))
    ]
    for copy in extras:
        copy.start()
    locals_ = [
        pltpu.make_async_copy(feat_ref, x_ref.at[:, :, 0:half], loc_sem.at[0]),
        pltpu.make_async_copy(cot_ref, c_ref.at[:, :, 0:half], loc_sem.at[1]),
    ]
    for copy in locals_:
        copy.start()

    def arrive(d, carry):
        peer_copy(d).wait_recv()
        forward(lax.rem(me - d + n, n)).start()
        return carry

    lax.fori_loop(1, n, arrive, 0)
    for copy in locals_:
        copy.wait()
    for copy in extras:
        copy.wait()

    def finish(d, carry):
        peer_copy(d).wait_send()
        return carry

    lax.fori_loop(1, n, finish, 0)

    def finish_forward(q, carry):
        forward(q).wait()
        return carry

    lax.fori_loop(0, n, finish_forward, 0)


def slot_loop(first, last, step):
    full = (last - first) // UNROLL

    def many(i, carry):
        for u in range(UNROLL):
            step(first + i * UNROLL + u)
        return carry

    lax.fori_loop(0, full, many, 0)

    def single(k, carry):
        step(k)
        return carry

    lax.fori_loop(first + full * UNROLL, last, single, 0)


def local_kernel(
    hub_dev, feat_ref, row_ref, owner_ref, count_ref,
    cols_ref, x_hbm, c_hbm, ws_ref, wn_ref, wso_ref, wno_ref, val_hbm, panel_ref,
    out_hbm, grad_ref, direct_hbm, terms_ref,
    acc, sq, slopes_t, terms_t, hub_s, x_ref, c_ref, val_ref, out_ref, direct_ref, w_ahead, w_back,
    val_sem, in_sem, out_sem, direct_sem,
):
    f = feat_ref[0]
    tiles, edge, wide = x_ref.shape
    half = wide // 2
    n = cols_ref.shape[0]
    hubs = panel_ref.shape[0]
    pad = cols_ref.shape[1] - edge
    parts = val_sem.shape[0]
    cap = val_ref.shape[0] // parts
    group = tiles // out_sem.shape[0]
    rows = group * edge
    count = count_ref[0]

    def val_copy(i):
        return pltpu.make_async_copy(
            val_hbm.at[pl.ds(i * cap, cap)], val_ref.at[pl.ds(i * cap, cap)], val_sem.at[i]
        )

    def out_copies(i):
        span = pl.ds(i * group, group)
        return (
            pltpu.make_async_copy(out_ref.at[span], out_hbm.at[span], out_sem.at[i]),
            pltpu.make_async_copy(direct_ref.at[span], direct_hbm.at[span], direct_sem.at[i]),
        )

    for i in range(parts):
        val_copy(i).start()
    x_copy = pltpu.make_async_copy(x_hbm, x_ref, in_sem.at[0])
    c_copy = pltpu.make_async_copy(c_hbm, c_ref, in_sem.at[1])
    x_copy.start()
    c_copy.start()

    def local_order(w):
        return jnp.where(f == 0, w, jnp.concatenate([w[:, half:], w[:, :half]], axis=1))

    ws_own = local_order(ws_ref[...].astype(F32))
    wn_own = local_order(wn_ref[...].astype(F32))
    ws_other = local_order(wso_ref[...].astype(F32))
    wn_other = local_order(wno_ref[...].astype(F32))
    w_ahead[...] = jnp.concatenate([ws_own, ws_other, wn_own, wn_other], axis=0).astype(BF16)
    w_back[...] = jnp.concatenate([ws_own, wn_own], axis=0).T.astype(BF16)

    hub_ids = lax.broadcasted_iota(jnp.int32, (hubs, n * pad), 0)
    place = lax.broadcasted_iota(jnp.int32, (hubs, n * pad), 1)
    pick = (hub_ids // hub_dev == place // pad) & (hub_ids % hub_dev == place % pad)
    hub_rows = cols_ref[:, edge:, :].reshape(n * pad, wide)
    hub_feats = dot(jnp.where(pick, 1.0, 0.0).astype(BF16), hub_rows).astype(BF16)

    def panel_part(i):
        return panel_ref[:, pl.ds(pl.multiple_of(i * rows, rows), rows)]

    def start(i, carry):
        panel = panel_part(i).astype(F32).T
        span = pl.ds(i * group, group)
        acc[span] = dot(panel.astype(BF16), hub_feats).reshape(group, edge, wide)
        squares = panel * panel
        if hubs < edge:
            squares = jnp.concatenate([squares, jnp.zeros((rows, edge - hubs), F32)], axis=1)
        else:
            squares = sum(squares[:, j:j + edge] for j in range(0, hubs, edge))
        sq[span] = squares.reshape(group, edge, edge)
        return carry

    lax.fori_loop(0, tiles // group, start, 0)

    def ahead(k):
        values = val_ref[k]
        row = row_ref[k]
        acc[row] += dot(values, cols_ref[owner_ref[k], 0:edge, :])
        wide_values = values.astype(F32)
        sq[row] += wide_values * wide_values

    def part(i, carry):
        val_copy(i).wait()
        first = i * cap
        slot_loop(first, jnp.clip(count, first, first + cap), ahead)
        return carry

    lax.fori_loop(0, parts, part, 0)

    grad_ref[...] = jnp.zeros_like(grad_ref)
    hub_s[...] = jnp.zeros_like(hub_s)
    ones = jnp.ones((2 * edge, half), BF16)
    x_copy.wait()
    c_copy.wait()

    def dense(i, carry):
        span = pl.ds(i * group, group)
        squares = sq[span].reshape(rows, edge)
        high = squares.astype(BF16)
        low = (squares - high.astype(F32)).astype(BF16)
        inverse = lax.rsqrt(1.0 + dot(jnp.concatenate([high, low], axis=1), ones))
        x = x_ref[span].reshape(rows, wide)
        sums = acc[span].reshape(rows, wide)
        aggregate = (sums * jnp.concatenate([inverse, inverse], axis=1)).astype(BF16)
        preact = dot(jnp.concatenate([x, aggregate], axis=1), w_ahead[...])
        out_ref[span] = jnp.maximum(preact[:, :half], 0.0).astype(BF16).reshape(group, edge, half)
        cotangent = c_ref[span].reshape(rows, wide).astype(F32)
        slopes = jnp.where(preact > 0, cotangent, 0.0).astype(BF16)
        both = dot(slopes, w_back[...])
        direct_ref[span] = both[:, :half].reshape(group, edge, half)
        for copy in out_copies(i):
            copy.start()
        back = (both[:, half:] * inverse).astype(BF16)
        hub_s[...] += dot(panel_part(i), back)
        back_t = back.T
        for g in range(group):
            slopes_t[i * group + g] = back_t[:, g * edge:(g + 1) * edge]
        left = jnp.concatenate([x[:, :half], aggregate[:, :half]], axis=1)
        grad_ref[...] += dot(left, slopes, ((0,), (0,)))
        return carry

    lax.fori_loop(0, tiles // group, dense, 0)

    def clear(o, carry):
        terms_t[o] = jnp.zeros((half, edge), F32)
        return carry

    lax.fori_loop(0, n, clear, 0)

    def behind(k):
        terms_t[owner_ref[k]] += dot(slopes_t[row_ref[k]], val_ref[k])

    slot_loop(0, count, behind)

    hub_terms = hub_s[...]
    high = hub_terms.astype(BF16)
    low = (hub_terms - high.astype(F32)).astype(BF16)
    ids = lax.broadcasted_iota(jnp.int32, (n * pad, hubs), 1)
    spot = lax.broadcasted_iota(jnp.int32, (n * pad, hubs), 0)
    same = ids // hub_dev == spot // pad
    put_high = jnp.where(same & (spot % pad == ids % hub_dev), 1.0, 0.0).astype(BF16)
    put_low = jnp.where(same & (spot % pad == ids % hub_dev + hub_dev), 1.0, 0.0).astype(BF16)
    blocks = dot(put_high, high) + dot(put_low, low)
    terms_ref[:, edge:, :] = blocks.reshape(n, pad, half).astype(BF16)

    def emit(o, carry):
        terms_ref[o, 0:edge, :] = terms_t[o].T.astype(BF16)
        return carry

    lax.fori_loop(0, n, emit, 0)

    def drain(i, carry):
        for copy in out_copies(i):
            copy.wait()
        return carry

    lax.fori_loop(0, tiles // group, drain, 0)


def return_kernel(n, reduce_here, factor, *refs):
    if reduce_here:
        (terms_ref, grad_ref, back_ref, self_ref, neigh_ref,
         send_sem, recv_sem, gstage, gin, gall, rsend, rrecv, asend, arecv) = refs
    else:
        terms_ref, back_ref, send_sem, recv_sem = refs
    me = lax.axis_index("dom")
    feat = lax.axis_index("feat")
    greet(n, me, feat, False)

    def copy_to(d, src, dst, ssem, rsem):
        return pltpu.make_async_remote_copy(
            src_ref=src, dst_ref=dst, send_sem=ssem.at[d], recv_sem=rsem.at[d],
            device_id={"dom": lax.rem(me + d, n)}, device_id_type=pl.DeviceIdType.MESH,
        )

    def term_copy(d):
        return copy_to(d, terms_ref.at[lax.rem(me + d, n)], back_ref.at[me], send_sem, recv_sem)

    def each(fn):
        def body(d, carry):
            fn(d)
            return carry
        lax.fori_loop(1, n, body, 0)

    if reduce_here:
        piece = grad_ref.shape[0] // n

        def part_copy(d):
            return copy_to(d, gstage.at[lax.rem(me + d, n)], gin.at[me], rsend, rrecv)

        def all_copy(d):
            return copy_to(d, gall.at[me], gall.at[me], asend, arecv)

        gstage[...] = grad_ref[...].astype(BF16).reshape(gstage.shape)
        each(lambda d: part_copy(d).start())
    each(lambda d: term_copy(d).start())
    back_ref[me] = terms_ref[me]
    if reduce_here:
        gin[me] = gstage[me]
        each(lambda d: part_copy(d).wait_recv())
        gall[me] = jnp.sum(gin[...].astype(F32), axis=0).astype(BF16)
        each(lambda d: all_copy(d).start())
    each(lambda d: term_copy(d).wait())
    if reduce_here:
        each(lambda d: part_copy(d).wait_send())
        each(lambda d: all_copy(d).wait())
        total = gall[...].astype(F32).reshape(grad_ref.shape) * factor
        half = total.shape[1] // 2
        total = jnp.where(feat == 0, total, jnp.concatenate([total[:, half:], total[:, :half]], axis=1))
        self_ref[...] = total[: self_ref.shape[0]]
        neigh_ref[...] = total[self_ref.shape[0]:]


def finish_kernel(hub_dev, send_ref, hub_ref, direct_ref, back_ref, out_ref):
    n = back_ref.shape[0]
    edge = 128
    out_ref[...] = direct_ref[...]

    def add(q, carry):
        rows = pl.ds(pl.multiple_of(send_ref[q] * edge, edge), edge)
        out_ref[rows, :] += back_ref[q, 0:edge, :].astype(F32)
        return carry

    lax.fori_loop(0, n, add, 0)

    def gather(q, total):
        return total + back_ref[q, edge:, :].astype(F32)

    total = lax.fori_loop(0, n, gather, jnp.zeros((back_ref.shape[1] - edge, back_ref.shape[2]), F32))
    for h in range(hub_dev):
        row = total[h:h + 1] + total[hub_dev + h:hub_dev + h + 1]
        out_ref[pl.ds(hub_ref[h], 1), :] += row


def shards(
    features, self_weight, neighbor_weight, tile_values, tile_row, tile_owner,
    send_tile, tile_count, hub_panel, hub_rows, cotangent,
):
    rows, half = features.shape
    edge = tile_values.shape[1]
    tiles = rows // edge
    n = lax.axis_size("dom")
    hub_dev = hub_rows.shape[0]
    hubs = hub_panel.shape[1]
    wide = 2 * half
    pad = -(-2 * hub_dev // 16) * 16
    tall = edge + pad
    sds = jax.ShapeDtypeStruct
    dma = pltpu.SemaphoreType.DMA
    params = functools.partial(pltpu.CompilerParams, vmem_limit_bytes=VMEM_BYTES)

    cols, x_all, c_all, ws_other, wn_other = pl.pallas_call(
        functools.partial(exchange_kernel, n, hub_dev),
        out_shape=(
            sds((n, tall, wide), BF16), sds((tiles, edge, wide), BF16), sds((tiles, edge, wide), BF16),
            sds(self_weight.shape, BF16), sds(neighbor_weight.shape, BF16),
        ),
        in_specs=[vmem()] * 4 + [smem()] * 2,
        out_specs=(vmem(),) * 5,
        scratch_shapes=[
            pltpu.VMEM((n, tall, half), BF16),
            dma((n,)), dma((n,)), dma((n,)), dma((n,)), dma((2,)), dma((4,)), dma((4,)),
        ],
        compiler_params=params(collective_id=0, has_side_effects=True),
        name="exchange",
    )(
        features.reshape(tiles, edge, half), cotangent.reshape(tiles, edge, half),
        self_weight, neighbor_weight, send_tile, hub_rows,
    )

    feat_index = lax.axis_index("feat").astype(jnp.int32).reshape(1)
    anywhere = pl.BlockSpec(memory_space=pl.ANY)
    slots = tile_values.shape[0]
    parts = math.gcd(slots, 8)
    chunks = tiles // math.gcd(tiles, 4)
    layer, grads, direct, terms = pl.pallas_call(
        functools.partial(local_kernel, hub_dev),
        out_shape=(
            sds((tiles, edge, half), BF16), sds((wide, wide), F32),
            sds((tiles, edge, half), F32), sds((n, tall, half), BF16),
        ),
        in_specs=[smem()] * 4 + [vmem(), anywhere, anywhere] + [vmem()] * 4 + [anywhere, vmem()],
        out_specs=(anywhere, vmem(), anywhere, vmem()),
        scratch_shapes=[
            pltpu.VMEM((tiles, edge, wide), F32),
            pltpu.VMEM((tiles, edge, edge), F32),
            pltpu.VMEM((tiles, half, edge), BF16),
            pltpu.VMEM((n, half, edge), F32),
            pltpu.VMEM((hubs, half), F32),
            pltpu.VMEM((tiles, edge, wide), BF16),
            pltpu.VMEM((tiles, edge, wide), BF16),
            pltpu.VMEM(tile_values.shape, BF16),
            pltpu.VMEM((tiles, edge, half), BF16),
            pltpu.VMEM((tiles, edge, half), F32),
            pltpu.VMEM((2 * wide, wide), BF16),
            pltpu.VMEM((wide, wide), BF16),
            dma((parts,)), dma((2,)), dma((chunks,)), dma((chunks,)),
        ],
        compiler_params=params(),
        name="local_pass",
    )(
        feat_index, tile_row, tile_owner, tile_count, cols, x_all, c_all,
        self_weight, neighbor_weight, ws_other, wn_other, tile_values, hub_panel.T,
    )

    factor = 1.0 / math.sqrt(rows * n)
    reduce_here = wide % (16 * n) == 0
    back_shape = sds((n, tall, half), BF16)
    if reduce_here:
        part = (n, wide // n, wide)
        back, self_grad, neighbor_grad = pl.pallas_call(
            functools.partial(return_kernel, n, True, factor),
            out_shape=(back_shape, sds((half, wide), F32), sds((half, wide), F32)),
            in_specs=[vmem()] * 2,
            out_specs=(vmem(),) * 3,
            scratch_shapes=[dma((n,)), dma((n,))] + [pltpu.VMEM(part, BF16)] * 3 + [dma((n,))] * 4,
            compiler_params=params(collective_id=1, has_side_effects=True),
            name="send_back",
        )(terms, grads)
    else:
        back = pl.pallas_call(
            functools.partial(return_kernel, n, False, factor),
            out_shape=back_shape,
            in_specs=[vmem()],
            out_specs=vmem(),
            scratch_shapes=[dma((n,)), dma((n,))],
            compiler_params=params(collective_id=1, has_side_effects=True),
            name="send_back",
        )(terms)
        total = lax.psum(grads, "dom") * factor
        swapped = jnp.concatenate([total[:, half:], total[:, :half]], axis=1)
        total = jnp.where(feat_index[0] == 0, total, swapped)
        self_grad, neighbor_grad = total[:half], total[half:]

    input_grad = pl.pallas_call(
        functools.partial(finish_kernel, hub_dev),
        out_shape=sds((rows, half), F32),
        in_specs=[smem()] * 2 + [vmem()] * 2,
        out_specs=vmem(),
        compiler_params=params(),
        name="finish",
    )(send_tile, hub_rows, direct.reshape(rows, half), back)
    return layer.reshape(rows, half), self_grad, neighbor_grad, input_grad


def solution(mesh):
    placed = (
        P("dom", "feat"), P("feat", None), P("feat", None), P("dom", None, None), P("dom"), P("dom"),
        P("dom"), P("dom"), P("dom", None), P("dom"), P("dom", "feat"),
    )
    return jax.shard_map(
        shards,
        mesh=mesh,
        in_specs=placed,
        out_specs=(P("dom", "feat"), P("feat", None), P("feat", None), P("dom", "feat")),
        check_vma=False,
    )
```

```python
import functools
import math

import jax
import jax.numpy as jnp
from jax import lax
from jax.experimental import pallas as pl
from jax.experimental.pallas import tpu as pltpu
from jax.sharding import PartitionSpec as P

F32 = jnp.float32
BF16 = jnp.bfloat16
VMEM_BYTES = 58 * 2**20
UNROLL = 8


def vmem():
    return pl.BlockSpec(memory_space=pltpu.VMEM)


def smem():
    return pl.BlockSpec(memory_space=pltpu.SMEM)


def dot(a, b, dims=((1,), (0,))):
    return lax.dot_general(a, b, (dims, ((), ())), preferred_element_type=F32)


def greet(n, me, feat, with_sibling):
    barrier = pltpu.get_barrier_semaphore()

    def hello(d, carry):
        pl.semaphore_signal(
            barrier, inc=1, device_id={"dom": lax.rem(me + d, n)}, device_id_type=pl.DeviceIdType.MESH
        )
        return carry

    lax.fori_loop(1, n, hello, 0)
    if with_sibling:
        pl.semaphore_signal(barrier, inc=1, device_id={"feat": 1 - feat}, device_id_type=pl.DeviceIdType.MESH)


def wait_greetings(count):
    pl.semaphore_wait(pltpu.get_barrier_semaphore(), count)


def exchange_kernel(
    n, hub_dev, feat_ref, cot_ref, ws_ref, wn_ref, send_ref, hub_ref,
    cols_ref, x_ref, c_ref, wso_ref, wno_ref,
    stage, send_sem, recv_sem, fsend_sem, frecv_sem, loc_sem, esend_sem, erecv_sem,
):
    me = lax.axis_index("dom")
    feat = lax.axis_index("feat")
    edge = feat_ref.shape[1]
    rows = edge * feat_ref.shape[0]
    pad = stage.shape[1] - edge
    half = feat_ref.shape[2]
    greet(n, me, feat, True)

    row_ids = lax.broadcasted_iota(jnp.int32, (edge, half), 0)
    out_ids = lax.broadcasted_iota(jnp.int32, (pad, half), 0)
    hub_block = jnp.zeros((pad, half), F32)
    for h in range(hub_dev):
        r = hub_ref[h]
        tile = feat_ref[r // edge].astype(F32)
        row = jnp.sum(jnp.where(row_ids == r % edge, tile, 0.0), axis=0, keepdims=True)
        hub_block = jnp.where(out_ids == h, row, hub_block)
    hub_block = hub_block.astype(BF16)

    def fill(d, carry):
        stage[d, 0:edge, :] = feat_ref[send_ref[lax.rem(me + d, n)]]
        stage[d, edge:, :] = hub_block
        return carry

    lax.fori_loop(1, n, fill, 0)
    cols_ref[me, 0:edge, 0:half] = feat_ref[send_ref[me]]
    cols_ref[me, edge:, 0:half] = hub_block
    wait_greetings(n)

    def peer_copy(d):
        return pltpu.make_async_remote_copy(
            src_ref=stage.at[d], dst_ref=cols_ref.at[me, :, 0:half],
            send_sem=send_sem.at[d], recv_sem=recv_sem.at[d],
            device_id={"dom": lax.rem(me + d, n)}, device_id_type=pl.DeviceIdType.MESH,
        )

    def forward(q):
        return pltpu.make_async_remote_copy(
            src_ref=cols_ref.at[q, :, 0:half], dst_ref=cols_ref.at[q, :, half:2 * half],
            send_sem=fsend_sem.at[q], recv_sem=frecv_sem.at[q],
            device_id={"feat": 1 - feat}, device_id_type=pl.DeviceIdType.MESH,
        )

    def send(d, carry):
        peer_copy(d).start()
        return carry

    lax.fori_loop(1, n, send, 0)
    forward(me).start()

    extras = [
        pltpu.make_async_remote_copy(
            src_ref=src, dst_ref=dst, send_sem=esend_sem.at[i], recv_sem=erecv_sem.at[i],
            device_id={"feat": 1 - feat}, device_id_type=pl.DeviceIdType.MESH,
        )
        for i, (src, dst) in enumerate((
            (feat_ref, x_ref.at[:, :, half:2 * half]),
            (cot_ref, c_ref.at[:, :, half:2 * half]),
            (ws_ref, wso_ref),
            (wn_ref, wno_ref),
        ))
    ]
    for copy in extras:
        copy.start()
    locals_ = [
        pltpu.make_async_copy(feat_ref, x_ref.at[:, :, 0:half], loc_sem.at[0]),
        pltpu.make_async_copy(cot_ref, c_ref.at[:, :, 0:half], loc_sem.at[1]),
    ]
    for copy in locals_:
        copy.start()

    def arrive(d, carry):
        peer_copy(d).wait_recv()
        forward(lax.rem(me - d + n, n)).start()
        return carry

    lax.fori_loop(1, n, arrive, 0)
    for copy in locals_:
        copy.wait()
    for copy in extras:
        copy.wait()

    def finish(d, carry):
        peer_copy(d).wait_send()
        return carry

    lax.fori_loop(1, n, finish, 0)

    def finish_forward(q, carry):
        forward(q).wait()
        return carry

    lax.fori_loop(0, n, finish_forward, 0)


def slot_loop(first, last, step):
    full = (last - first) // UNROLL

    def many(i, carry):
        for u in range(UNROLL):
            step(first + i * UNROLL + u)
        return carry

    lax.fori_loop(0, full, many, 0)

    def single(k, carry):
        step(k)
        return carry

    lax.fori_loop(first + full * UNROLL, last, single, 0)


def local_kernel(
    hub_dev, feat_ref, row_ref, owner_ref, count_ref,
    cols_ref, x_hbm, c_hbm, ws_ref, wn_ref, wso_ref, wno_ref, val_hbm, panel_ref,
    out_hbm, grad_ref, direct_hbm, terms_ref,
    acc, sq, slopes_t, terms_t, hub_s, x_ref, c_ref, val_ref, out_ref, direct_ref, w_ahead, w_back,
    val_sem, in_sem, out_sem, direct_sem,
):
    f = feat_ref[0]
    tiles, edge, wide = x_ref.shape
    half = wide // 2
    n = cols_ref.shape[0]
    hubs = panel_ref.shape[0]
    pad = cols_ref.shape[1] - edge
    parts = val_sem.shape[0]
    cap = val_ref.shape[0] // parts
    group = tiles // out_sem.shape[0]
    rows = group * edge
    count = count_ref[0]

    def val_copy(i):
        return pltpu.make_async_copy(
            val_hbm.at[pl.ds(i * cap, cap)], val_ref.at[pl.ds(i * cap, cap)], val_sem.at[i]
        )

    def out_copies(i):
        span = pl.ds(i * group, group)
        return (
            pltpu.make_async_copy(out_ref.at[span], out_hbm.at[span], out_sem.at[i]),
            pltpu.make_async_copy(direct_ref.at[span], direct_hbm.at[span], direct_sem.at[i]),
        )

    for i in range(parts):
        val_copy(i).start()
    x_copy = pltpu.make_async_copy(x_hbm, x_ref, in_sem.at[0])
    c_copy = pltpu.make_async_copy(c_hbm, c_ref, in_sem.at[1])
    x_copy.start()
    c_copy.start()

    def local_order(w):
        return jnp.where(f == 0, w, jnp.concatenate([w[:, half:], w[:, :half]], axis=1))

    ws_own = local_order(ws_ref[...].astype(F32))
    wn_own = local_order(wn_ref[...].astype(F32))
    ws_other = local_order(wso_ref[...].astype(F32))
    wn_other = local_order(wno_ref[...].astype(F32))
    w_ahead[...] = jnp.concatenate([ws_own, ws_other, wn_own, wn_other], axis=0).astype(BF16)
    w_back[...] = jnp.concatenate([ws_own, wn_own], axis=0).T.astype(BF16)

    hub_ids = lax.broadcasted_iota(jnp.int32, (hubs, n * pad), 0)
    place = lax.broadcasted_iota(jnp.int32, (hubs, n * pad), 1)
    pick = (hub_ids // hub_dev == place // pad) & (hub_ids % hub_dev == place % pad)
    hub_rows = cols_ref[:, edge:, :].reshape(n * pad, wide)
    hub_feats = dot(jnp.where(pick, 1.0, 0.0).astype(BF16), hub_rows).astype(BF16)

    def panel_part(i):
        return panel_ref[:, pl.ds(pl.multiple_of(i * rows, rows), rows)]

    def start(i, carry):
        panel = panel_part(i).astype(F32).T
        span = pl.ds(i * group, group)
        acc[span] = dot(panel.astype(BF16), hub_feats).reshape(group, edge, wide)
        squares = panel * panel
        if hubs < edge:
            squares = jnp.concatenate([squares, jnp.zeros((rows, edge - hubs), F32)], axis=1)
        else:
            squares = sum(squares[:, j:j + edge] for j in range(0, hubs, edge))
        sq[span] = squares.reshape(group, edge, edge)
        return carry

    lax.fori_loop(0, tiles // group, start, 0)

    def ahead(k):
        values = val_ref[k]
        row = row_ref[k]
        acc[row] += dot(values, cols_ref[owner_ref[k], 0:edge, :])
        wide_values = values.astype(F32)
        sq[row] += wide_values * wide_values

    def part(i, carry):
        val_copy(i).wait()
        first = i * cap
        slot_loop(first, jnp.clip(count, first, first + cap), ahead)
        return carry

    lax.fori_loop(0, parts, part, 0)

    grad_ref[...] = jnp.zeros_like(grad_ref)
    hub_s[...] = jnp.zeros_like(hub_s)
    ones = jnp.ones((2 * edge, half), BF16)
    x_copy.wait()
    c_copy.wait()

    def dense(i, carry):
        span = pl.ds(i * group, group)
        squares = sq[span].reshape(rows, edge)
        high = squares.astype(BF16)
        low = (squares - high.astype(F32)).astype(BF16)
        inverse = lax.rsqrt(1.0 + dot(jnp.concatenate([high, low], axis=1), ones))
        x = x_ref[span].reshape(rows, wide)
        sums = acc[span].reshape(rows, wide)
        aggregate = (sums * jnp.concatenate([inverse, inverse], axis=1)).astype(BF16)
        preact = dot(jnp.concatenate([x, aggregate], axis=1), w_ahead[...])
        out_ref[span] = jnp.maximum(preact[:, :half], 0.0).astype(BF16).reshape(group, edge, half)
        cotangent = c_ref[span].reshape(rows, wide).astype(F32)
        slopes = jnp.where(preact > 0, cotangent, 0.0).astype(BF16)
        both = dot(slopes, w_back[...])
        direct_ref[span] = both[:, :half].reshape(group, edge, half)
        for copy in out_copies(i):
            copy.start()
        back = (both[:, half:] * inverse).astype(BF16)
        hub_s[...] += dot(panel_part(i), back)
        back_t = back.T
        for g in range(group):
            slopes_t[i * group + g] = back_t[:, g * edge:(g + 1) * edge]
        left = jnp.concatenate([x[:, :half], aggregate[:, :half]], axis=1)
        grad_ref[...] += dot(left, slopes, ((0,), (0,)))
        return carry

    lax.fori_loop(0, tiles // group, dense, 0)

    def clear(o, carry):
        terms_t[o] = jnp.zeros((half, edge), F32)
        return carry

    lax.fori_loop(0, n, clear, 0)

    def behind(k):
        terms_t[owner_ref[k]] += dot(slopes_t[row_ref[k]], val_ref[k])

    slot_loop(0, count, behind)

    hub_terms = hub_s[...]
    high = hub_terms.astype(BF16)
    low = (hub_terms - high.astype(F32)).astype(BF16)
    ids = lax.broadcasted_iota(jnp.int32, (n * pad, hubs), 1)
    spot = lax.broadcasted_iota(jnp.int32, (n * pad, hubs), 0)
    same = ids // hub_dev == spot // pad
    put_high = jnp.where(same & (spot % pad == ids % hub_dev), 1.0, 0.0).astype(BF16)
    put_low = jnp.where(same & (spot % pad == ids % hub_dev + hub_dev), 1.0, 0.0).astype(BF16)
    blocks = dot(put_high, high) + dot(put_low, low)
    terms_ref[:, edge:, :] = blocks.reshape(n, pad, half).astype(BF16)

    def emit(o, carry):
        terms_ref[o, 0:edge, :] = terms_t[o].T.astype(BF16)
        return carry

    lax.fori_loop(0, n, emit, 0)

    def drain(i, carry):
        for copy in out_copies(i):
            copy.wait()
        return carry

    lax.fori_loop(0, tiles // group, drain, 0)


def return_kernel(n, inner, factor, *refs):
    if inner:
        (terms_ref, grad_ref, back_ref, self_ref, neigh_ref,
         send_sem, recv_sem, gstage, gin, hstage, hin, gall, step_send, step_recv) = refs
    else:
        terms_ref, back_ref, send_sem, recv_sem = refs
    me = lax.axis_index("dom")
    feat = lax.axis_index("feat")
    greet(n, me, feat, False)
    if inner:
        gstage[...] = grad_ref[...].astype(BF16).reshape(gstage.shape)
    back_ref[me] = terms_ref[me]
    wait_greetings(n - 1)

    def copy_to(target, src, dst, ssem, rsem):
        return pltpu.make_async_remote_copy(
            src_ref=src, dst_ref=dst, send_sem=ssem, recv_sem=rsem,
            device_id={"dom": target}, device_id_type=pl.DeviceIdType.MESH,
        )

    def term_copy(d):
        q = lax.rem(me + d, n)
        return copy_to(q, terms_ref.at[q], back_ref.at[me], send_sem.at[d], recv_sem.at[d])

    def each(fn, size):
        def body(d, carry):
            fn(d)
            return carry
        lax.fori_loop(1, size, body, 0)

    if inner:
        outer = n // inner
        z, i = me // inner, lax.rem(me, inner)

        def plane_copy(d, phase, src, dst):
            j = lax.rem(i + d, inner)
            return copy_to(z * inner + j, src(j), dst, step_send.at[phase, d], step_recv.at[phase, d])

        def line_copy(d, phase, src, dst):
            k = lax.rem(z + d, outer)
            return copy_to(k * inner + i, src(k), dst, step_send.at[phase, d], step_recv.at[phase, d])

        def scatter_plane(d):
            return plane_copy(d, 0, lambda j: gstage.at[j], gin.at[i])

        def scatter_line(d):
            return line_copy(d, 1, lambda k: hstage.at[k], hin.at[z])

        def gather_line(d):
            return line_copy(d, 2, lambda k: gall.at[i, z], gall.at[i, z])

        def gather_plane(d):
            return plane_copy(d, 3, lambda j: gall.at[i], gall.at[i])

        each(lambda d: scatter_plane(d).start(), inner)
    each(lambda d: term_copy(d).start(), n)
    if inner:
        gin[i] = gstage[i]
        each(lambda d: scatter_plane(d).wait_recv(), inner)
        hstage[...] = jnp.sum(gin[...].astype(F32), axis=0).astype(BF16)
        each(lambda d: scatter_line(d).start(), outer)
        hin[z] = hstage[z]
        each(lambda d: scatter_line(d).wait_recv(), outer)
        gall[i, z] = jnp.sum(hin[...].astype(F32), axis=0).astype(BF16)
        each(lambda d: gather_line(d).start(), outer)
        each(lambda d: gather_line(d).wait_recv(), outer)
        each(lambda d: gather_plane(d).start(), inner)
    each(lambda d: term_copy(d).wait(), n)
    if inner:
        each(lambda d: scatter_plane(d).wait_send(), inner)
        each(lambda d: scatter_line(d).wait_send(), outer)
        each(lambda d: gather_line(d).wait_send(), outer)
        each(lambda d: gather_plane(d).wait(), inner)
        total = gall[...].astype(F32).reshape(grad_ref.shape) * factor
        half = total.shape[1] // 2
        total = jnp.where(feat == 0, total, jnp.concatenate([total[:, half:], total[:, :half]], axis=1))
        self_ref[...] = total[: self_ref.shape[0]]
        neigh_ref[...] = total[self_ref.shape[0]:]


def finish_kernel(hub_dev, edge, send_ref, hub_ref, direct_ref, back_ref, out_ref):
    n = back_ref.shape[0]
    span = out_ref.shape[0]
    base = pl.program_id(0) * span
    out_ref[...] = direct_ref[...]

    def add(q, carry):
        place = send_ref[q] * edge - base

        @pl.when((place >= 0) & (place < span))
        def _():
            rows = pl.ds(pl.multiple_of(place, edge), edge)
            out_ref[rows, :] += back_ref[q, 0:edge, :].astype(F32)

        return carry

    lax.fori_loop(0, n, add, 0)
    for h in range(hub_dev):
        place = hub_ref[h] - base

        @pl.when((place >= 0) & (place < span))
        def _():
            total = jnp.sum(back_ref[:, edge:, :].astype(F32), axis=0)
            row = total[h:h + 1] + total[hub_dev + h:hub_dev + h + 1]
            out_ref[pl.ds(place, 1), :] += row


def shards(
    features, self_weight, neighbor_weight, tile_values, tile_row, tile_owner,
    send_tile, tile_count, hub_panel, hub_rows, cotangent,
):
    rows, half = features.shape
    edge = tile_values.shape[1]
    tiles = rows // edge
    n = lax.axis_size("dom")
    hub_dev = hub_rows.shape[0]
    hubs = hub_panel.shape[1]
    wide = 2 * half
    pad = -(-2 * hub_dev // 16) * 16
    tall = edge + pad
    sds = jax.ShapeDtypeStruct
    dma = pltpu.SemaphoreType.DMA
    anywhere = pl.BlockSpec(memory_space=pl.ANY)
    params = functools.partial(pltpu.CompilerParams, vmem_limit_bytes=VMEM_BYTES)

    cols, x_all, c_all, ws_other, wn_other = pl.pallas_call(
        functools.partial(exchange_kernel, n, hub_dev),
        out_shape=(
            sds((n, tall, wide), BF16), sds((tiles, edge, wide), BF16), sds((tiles, edge, wide), BF16),
            sds(self_weight.shape, BF16), sds(neighbor_weight.shape, BF16),
        ),
        in_specs=[vmem(), anywhere, vmem(), vmem()] + [smem()] * 2,
        out_specs=(vmem(), anywhere, anywhere, vmem(), vmem()),
        scratch_shapes=[
            pltpu.VMEM((n, tall, half), BF16),
            dma((n,)), dma((n,)), dma((n,)), dma((n,)), dma((2,)), dma((4,)), dma((4,)),
        ],
        compiler_params=params(collective_id=0, has_side_effects=True),
        name="exchange",
    )(
        features.reshape(tiles, edge, half), cotangent.reshape(tiles, edge, half),
        self_weight, neighbor_weight, send_tile, hub_rows,
    )

    feat_index = lax.axis_index("feat").astype(jnp.int32).reshape(1)
    slots = tile_values.shape[0]
    parts = math.gcd(slots, 8)
    chunks = tiles // math.gcd(tiles, 4)
    layer, grads, direct, terms = pl.pallas_call(
        functools.partial(local_kernel, hub_dev),
        out_shape=(
            sds((tiles, edge, half), BF16), sds((wide, wide), F32),
            sds((tiles, edge, half), F32), sds((n, tall, half), BF16),
        ),
        in_specs=[smem()] * 4 + [vmem(), anywhere, anywhere] + [vmem()] * 4 + [anywhere, vmem()],
        out_specs=(anywhere, vmem(), anywhere, vmem()),
        scratch_shapes=[
            pltpu.VMEM((tiles, edge, wide), F32),
            pltpu.VMEM((tiles, edge, edge), F32),
            pltpu.VMEM((tiles, half, edge), BF16),
            pltpu.VMEM((n, half, edge), F32),
            pltpu.VMEM((hubs, half), F32),
            pltpu.VMEM((tiles, edge, wide), BF16),
            pltpu.VMEM((tiles, edge, wide), BF16),
            pltpu.VMEM(tile_values.shape, BF16),
            pltpu.VMEM((tiles, edge, half), BF16),
            pltpu.VMEM((tiles, edge, half), F32),
            pltpu.VMEM((2 * wide, wide), BF16),
            pltpu.VMEM((wide, wide), BF16),
            dma((parts,)), dma((2,)), dma((chunks,)), dma((chunks,)),
        ],
        compiler_params=params(),
        name="local_pass",
    )(
        feat_index, tile_row, tile_owner, tile_count, cols, x_all, c_all,
        self_weight, neighbor_weight, ws_other, wn_other, tile_values, hub_panel.T,
    )

    factor = 1.0 / math.sqrt(rows * n)
    inner = math.isqrt(n)
    if inner * inner != n or wide % (16 * n):
        inner = 0
    back_shape = sds((n, tall, half), BF16)
    if inner:
        line = (inner, wide // n, wide)
        back, self_grad, neighbor_grad = pl.pallas_call(
            functools.partial(return_kernel, n, inner, factor),
            out_shape=(back_shape, sds((half, wide), F32), sds((half, wide), F32)),
            in_specs=[vmem()] * 2,
            out_specs=(vmem(),) * 3,
            scratch_shapes=[
                dma((n,)), dma((n,)),
                pltpu.VMEM((inner,) + line, BF16), pltpu.VMEM((inner,) + line, BF16),
                pltpu.VMEM(line, BF16), pltpu.VMEM(line, BF16),
                pltpu.VMEM((inner,) + line, BF16),
                dma((4, inner)), dma((4, inner)),
            ],
            compiler_params=params(collective_id=1, has_side_effects=True),
            name="send_back",
        )(terms, grads)
    else:
        back = pl.pallas_call(
            functools.partial(return_kernel, n, 0, factor),
            out_shape=back_shape,
            in_specs=[vmem()],
            out_specs=vmem(),
            scratch_shapes=[dma((n,)), dma((n,))],
            compiler_params=params(collective_id=1, has_side_effects=True),
            name="send_back",
        )(terms)
        total = lax.psum(grads, "dom") * factor
        swapped = jnp.concatenate([total[:, half:], total[:, :half]], axis=1)
        total = jnp.where(feat_index[0] == 0, total, swapped)
        self_grad, neighbor_grad = total[:half], total[half:]

    steps = math.gcd(tiles, 4)
    block = pl.BlockSpec((rows // steps, half), lambda i: (i, 0))
    input_grad = pl.pallas_call(
        functools.partial(finish_kernel, hub_dev, edge),
        grid=(steps,),
        out_shape=sds((rows, half), F32),
        in_specs=[smem(), smem(), block, pl.BlockSpec((n, tall, half), lambda i: (0, 0, 0))],
        out_specs=block,
        compiler_params=params(),
        name="finish",
    )(send_tile, hub_rows, direct.reshape(rows, half), back)
    return layer.reshape(rows, half), self_grad, neighbor_grad, input_grad


def solution(mesh):
    placed = (
        P("dom", "feat"), P("feat", None), P("feat", None), P("dom", None, None), P("dom"), P("dom"),
        P("dom"), P("dom"), P("dom", None), P("dom"), P("dom", "feat"),
    )
    return jax.shard_map(
        shards,
        mesh=mesh,
        in_specs=placed,
        out_specs=(P("dom", "feat"), P("feat", None), P("feat", None), P("dom", "feat")),
        check_vma=False,
    )
```

```python
import functools
import math

import jax
import jax.numpy as jnp
from jax import lax
from jax.experimental import pallas as pl
from jax.experimental.pallas import tpu as pltpu
from jax.sharding import PartitionSpec as P

F32 = jnp.float32
BF16 = jnp.bfloat16
VMEM_BYTES = 58 * 2**20
UNROLL = 8


def vmem():
    return pl.BlockSpec(memory_space=pltpu.VMEM)


def smem():
    return pl.BlockSpec(memory_space=pltpu.SMEM)


def dot(a, b, dims=((1,), (0,))):
    return lax.dot_general(a, b, (dims, ((), ())), preferred_element_type=F32)


def greet(n, me, feat, with_sibling):
    barrier = pltpu.get_barrier_semaphore()

    def hello(d, carry):
        pl.semaphore_signal(
            barrier, inc=1, device_id={"dom": lax.rem(me + d, n)}, device_id_type=pl.DeviceIdType.MESH
        )
        return carry

    lax.fori_loop(1, n, hello, 0)
    if with_sibling:
        pl.semaphore_signal(barrier, inc=1, device_id={"feat": 1 - feat}, device_id_type=pl.DeviceIdType.MESH)


def wait_greetings(count):
    pl.semaphore_wait(pltpu.get_barrier_semaphore(), count)


def far_first(k, n):
    return lax.rem(n // 2 + lax.rem(k, 2) * (k + 1) // 2 - (1 - lax.rem(k, 2)) * (k // 2) + n, n)


def exchange_kernel(
    n, hub_dev, feat_ref, cot_ref, ws_ref, wn_ref, send_ref, hub_ref,
    cols_ref, x_ref, c_ref, wso_ref, wno_ref,
    stage, send_sem, recv_sem, fsend_sem, frecv_sem, loc_sem, esend_sem, erecv_sem,
):
    me = lax.axis_index("dom")
    feat = lax.axis_index("feat")
    edge = feat_ref.shape[1]
    rows = edge * feat_ref.shape[0]
    pad = stage.shape[1] - edge
    half = feat_ref.shape[2]
    greet(n, me, feat, True)

    row_ids = lax.broadcasted_iota(jnp.int32, (edge, half), 0)
    out_ids = lax.broadcasted_iota(jnp.int32, (pad, half), 0)
    hub_block = jnp.zeros((pad, half), F32)
    for h in range(hub_dev):
        r = hub_ref[h]
        tile = feat_ref[r // edge].astype(F32)
        row = jnp.sum(jnp.where(row_ids == r % edge, tile, 0.0), axis=0, keepdims=True)
        hub_block = jnp.where(out_ids == h, row, hub_block)
    hub_block = hub_block.astype(BF16)

    def fill(d, carry):
        stage[d, 0:edge, :] = feat_ref[send_ref[lax.rem(me + d, n)]]
        stage[d, edge:, :] = hub_block
        return carry

    lax.fori_loop(1, n, fill, 0)
    cols_ref[me, 0:edge, 0:half] = feat_ref[send_ref[me]]
    cols_ref[me, edge:, 0:half] = hub_block
    wait_greetings(n)

    def peer_copy(d):
        return pltpu.make_async_remote_copy(
            src_ref=stage.at[d], dst_ref=cols_ref.at[me, :, 0:half],
            send_sem=send_sem.at[d], recv_sem=recv_sem.at[d],
            device_id={"dom": lax.rem(me + d, n)}, device_id_type=pl.DeviceIdType.MESH,
        )

    def forward(q):
        return pltpu.make_async_remote_copy(
            src_ref=cols_ref.at[q, :, 0:half], dst_ref=cols_ref.at[q, :, half:2 * half],
            send_sem=fsend_sem.at[q], recv_sem=frecv_sem.at[q],
            device_id={"feat": 1 - feat}, device_id_type=pl.DeviceIdType.MESH,
        )

    def send(k, carry):
        peer_copy(far_first(k, n)).start()
        return carry

    lax.fori_loop(0, n - 1, send, 0)
    forward(me).start()

    extras = [
        pltpu.make_async_remote_copy(
            src_ref=src, dst_ref=dst, send_sem=esend_sem.at[i], recv_sem=erecv_sem.at[i],
            device_id={"feat": 1 - feat}, device_id_type=pl.DeviceIdType.MESH,
        )
        for i, (src, dst) in enumerate((
            (feat_ref, x_ref.at[:, :, half:2 * half]),
            (cot_ref, c_ref.at[:, :, half:2 * half]),
            (ws_ref, wso_ref),
            (wn_ref, wno_ref),
        ))
    ]
    for copy in extras:
        copy.start()
    locals_ = [
        pltpu.make_async_copy(feat_ref, x_ref.at[:, :, 0:half], loc_sem.at[0]),
        pltpu.make_async_copy(cot_ref, c_ref.at[:, :, 0:half], loc_sem.at[1]),
    ]
    for copy in locals_:
        copy.start()

    def arrive(d, carry):
        peer_copy(d).wait_recv()
        forward(lax.rem(me - d + n, n)).start()
        return carry

    lax.fori_loop(1, n, arrive, 0)
    for copy in locals_:
        copy.wait()
    for copy in extras:
        copy.wait()

    def finish(d, carry):
        peer_copy(d).wait_send()
        return carry

    lax.fori_loop(1, n, finish, 0)

    def finish_forward(q, carry):
        forward(q).wait()
        return carry

    lax.fori_loop(0, n, finish_forward, 0)


def slot_loop(first, last, step):
    full = (last - first) // UNROLL

    def many(i, carry):
        for u in range(UNROLL):
            step(first + i * UNROLL + u)
        return carry

    lax.fori_loop(0, full, many, 0)

    def single(k, carry):
        step(k)
        return carry

    lax.fori_loop(first + full * UNROLL, last, single, 0)


def local_kernel(
    hub_dev, feat_ref, row_ref, owner_ref, count_ref,
    cols_ref, x_hbm, c_hbm, ws_ref, wn_ref, wso_ref, wno_ref, val_hbm, panel_ref,
    out_hbm, grad_ref, direct_hbm, terms_ref,
    acc, sq, slopes_t, terms_t, hub_s, x_ref, c_ref, val_ref, out_ref, direct_ref, w_ahead, w_back,
    val_sem, in_sem, out_sem, direct_sem,
):
    f = feat_ref[0]
    tiles, edge, wide = x_ref.shape
    half = wide // 2
    n = cols_ref.shape[0]
    hubs = panel_ref.shape[0]
    pad = cols_ref.shape[1] - edge
    parts = val_sem.shape[0]
    cap = val_ref.shape[0] // parts
    group = tiles // out_sem.shape[0]
    rows = group * edge
    count = count_ref[0]

    def val_copy(i):
        return pltpu.make_async_copy(
            val_hbm.at[pl.ds(i * cap, cap)], val_ref.at[pl.ds(i * cap, cap)], val_sem.at[i]
        )

    def out_copies(i):
        span = pl.ds(i * group, group)
        return (
            pltpu.make_async_copy(out_ref.at[span], out_hbm.at[span], out_sem.at[i]),
            pltpu.make_async_copy(direct_ref.at[span], direct_hbm.at[span], direct_sem.at[i]),
        )

    for i in range(parts):
        val_copy(i).start()
    x_copy = pltpu.make_async_copy(x_hbm, x_ref, in_sem.at[0])
    c_copy = pltpu.make_async_copy(c_hbm, c_ref, in_sem.at[1])
    x_copy.start()
    c_copy.start()

    def local_order(w):
        return jnp.where(f == 0, w, jnp.concatenate([w[:, half:], w[:, :half]], axis=1))

    ws_own = local_order(ws_ref[...].astype(F32))
    wn_own = local_order(wn_ref[...].astype(F32))
    ws_other = local_order(wso_ref[...].astype(F32))
    wn_other = local_order(wno_ref[...].astype(F32))
    w_ahead[...] = jnp.concatenate([ws_own, ws_other, wn_own, wn_other], axis=0).astype(BF16)
    w_back[...] = jnp.concatenate([ws_own, wn_own], axis=0).T.astype(BF16)

    hub_ids = lax.broadcasted_iota(jnp.int32, (hubs, n * pad), 0)
    place = lax.broadcasted_iota(jnp.int32, (hubs, n * pad), 1)
    pick = (hub_ids // hub_dev == place // pad) & (hub_ids % hub_dev == place % pad)
    hub_rows = cols_ref[:, edge:, :].reshape(n * pad, wide)
    hub_feats = dot(jnp.where(pick, 1.0, 0.0).astype(BF16), hub_rows).astype(BF16)

    def panel_part(i):
        return panel_ref[:, pl.ds(pl.multiple_of(i * rows, rows), rows)]

    def start(i, carry):
        panel = panel_part(i).astype(F32).T
        span = pl.ds(i * group, group)
        acc[span] = dot(panel.astype(BF16), hub_feats).reshape(group, edge, wide)
        squares = panel * panel
        if hubs < edge:
            squares = jnp.concatenate([squares, jnp.zeros((rows, edge - hubs), F32)], axis=1)
        else:
            squares = sum(squares[:, j:j + edge] for j in range(0, hubs, edge))
        sq[span] = squares.reshape(group, edge, edge)
        return carry

    lax.fori_loop(0, tiles // group, start, 0)

    def ahead(k):
        values = val_ref[k]
        row = row_ref[k]
        acc[row] += dot(values, cols_ref[owner_ref[k], 0:edge, :])
        wide_values = values.astype(F32)
        sq[row] += wide_values * wide_values

    def part(i, carry):
        val_copy(i).wait()
        first = i * cap
        slot_loop(first, jnp.clip(count, first, first + cap), ahead)
        return carry

    lax.fori_loop(0, parts, part, 0)

    grad_ref[...] = jnp.zeros_like(grad_ref)
    hub_s[...] = jnp.zeros_like(hub_s)
    ones = jnp.ones((2 * edge, half), BF16)
    x_copy.wait()
    c_copy.wait()

    def dense(i, carry):
        span = pl.ds(i * group, group)
        squares = sq[span].reshape(rows, edge)
        high = squares.astype(BF16)
        low = (squares - high.astype(F32)).astype(BF16)
        inverse = lax.rsqrt(1.0 + dot(jnp.concatenate([high, low], axis=1), ones))
        x = x_ref[span].reshape(rows, wide)
        sums = acc[span].reshape(rows, wide)
        aggregate = (sums * jnp.concatenate([inverse, inverse], axis=1)).astype(BF16)
        preact = dot(jnp.concatenate([x, aggregate], axis=1), w_ahead[...])
        out_ref[span] = jnp.maximum(preact[:, :half], 0.0).astype(BF16).reshape(group, edge, half)
        cotangent = c_ref[span].reshape(rows, wide).astype(F32)
        slopes = jnp.where(preact > 0, cotangent, 0.0).astype(BF16)
        both = dot(slopes, w_back[...])
        direct_ref[span] = both[:, :half].reshape(group, edge, half)
        for copy in out_copies(i):
            copy.start()
        back = (both[:, half:] * inverse).astype(BF16)
        hub_s[...] += dot(panel_part(i), back)
        back_t = back.T
        for g in range(group):
            slopes_t[i * group + g] = back_t[:, g * edge:(g + 1) * edge]
        left = jnp.concatenate([x[:, :half], aggregate[:, :half]], axis=1)
        grad_ref[...] += dot(left, slopes, ((0,), (0,)))
        return carry

    lax.fori_loop(0, tiles // group, dense, 0)

    def clear(o, carry):
        terms_t[o] = jnp.zeros((half, edge), F32)
        return carry

    lax.fori_loop(0, n, clear, 0)

    def behind(k):
        terms_t[owner_ref[k]] += dot(slopes_t[row_ref[k]], val_ref[k])

    slot_loop(0, count, behind)

    hub_terms = hub_s[...]
    high = hub_terms.astype(BF16)
    low = (hub_terms - high.astype(F32)).astype(BF16)
    ids = lax.broadcasted_iota(jnp.int32, (n * pad, hubs), 1)
    spot = lax.broadcasted_iota(jnp.int32, (n * pad, hubs), 0)
    same = ids // hub_dev == spot // pad
    put_high = jnp.where(same & (spot % pad == ids % hub_dev), 1.0, 0.0).astype(BF16)
    put_low = jnp.where(same & (spot % pad == ids % hub_dev + hub_dev), 1.0, 0.0).astype(BF16)
    blocks = dot(put_high, high) + dot(put_low, low)
    terms_ref[:, edge:, :] = blocks.reshape(n, pad, half).astype(BF16)

    def emit(o, carry):
        terms_ref[o, 0:edge, :] = terms_t[o].T.astype(BF16)
        return carry

    lax.fori_loop(0, n, emit, 0)

    def drain(i, carry):
        for copy in out_copies(i):
            copy.wait()
        return carry

    lax.fori_loop(0, tiles // group, drain, 0)


def reduce_kernel(n, factor, grad_ref, self_ref, neigh_ref, gstage, gin, gall, rsend, rrecv, asend, arecv):
    me = lax.axis_index("dom")
    feat = lax.axis_index("feat")
    greet(n, me, feat, False)
    gstage[...] = grad_ref[...].astype(BF16).reshape(gstage.shape)
    gin[me] = gstage[me]
    wait_greetings(n - 1)

    def copy_to(d, src, dst, ssem, rsem):
        return pltpu.make_async_remote_copy(
            src_ref=src, dst_ref=dst, send_sem=ssem.at[d], recv_sem=rsem.at[d],
            device_id={"dom": lax.rem(me + d, n)}, device_id_type=pl.DeviceIdType.MESH,
        )

    def part_copy(d):
        return copy_to(d, gstage.at[lax.rem(me + d, n)], gin.at[me], rsend, rrecv)

    def all_copy(d):
        return copy_to(d, gall.at[me], gall.at[me], asend, arecv)

    def each(fn):
        def body(k, carry):
            fn(far_first(k, n))
            return carry
        lax.fori_loop(0, n - 1, body, 0)

    each(lambda d: part_copy(d).start())
    each(lambda d: part_copy(d).wait_recv())
    gall[me] = jnp.sum(gin[...].astype(F32), axis=0).astype(BF16)
    each(lambda d: all_copy(d).start())
    each(lambda d: part_copy(d).wait_send())
    each(lambda d: all_copy(d).wait())
    total = gall[...].astype(F32).reshape(grad_ref.shape) * factor
    half = total.shape[1] // 2
    total = jnp.where(feat == 0, total, jnp.concatenate([total[:, half:], total[:, :half]], axis=1))
    self_ref[...] = total[: self_ref.shape[0]]
    neigh_ref[...] = total[self_ref.shape[0]:]


def finish_kernel(hub_dev, send_ref, hub_ref, direct_ref, back_ref, out_ref):
    n = back_ref.shape[0]
    edge = 128
    out_ref[...] = direct_ref[...]

    def add(q, carry):
        rows = pl.ds(pl.multiple_of(send_ref[q] * edge, edge), edge)
        out_ref[rows, :] += back_ref[q, 0:edge, :].astype(F32)
        return carry

    lax.fori_loop(0, n, add, 0)

    def gather(q, total):
        return total + back_ref[q, edge:, :].astype(F32)

    total = lax.fori_loop(0, n, gather, jnp.zeros((back_ref.shape[1] - edge, back_ref.shape[2]), F32))
    for h in range(hub_dev):
        row = total[h:h + 1] + total[hub_dev + h:hub_dev + h + 1]
        out_ref[pl.ds(hub_ref[h], 1), :] += row


def shards(
    features, self_weight, neighbor_weight, tile_values, tile_row, tile_owner,
    send_tile, tile_count, hub_panel, hub_rows, cotangent,
):
    rows, half = features.shape
    edge = tile_values.shape[1]
    tiles = rows // edge
    n = lax.axis_size("dom")
    hub_dev = hub_rows.shape[0]
    hubs = hub_panel.shape[1]
    wide = 2 * half
    pad = -(-2 * hub_dev // 16) * 16
    tall = edge + pad
    sds = jax.ShapeDtypeStruct
    dma = pltpu.SemaphoreType.DMA
    params = functools.partial(pltpu.CompilerParams, vmem_limit_bytes=VMEM_BYTES)

    cols, x_all, c_all, ws_other, wn_other = pl.pallas_call(
        functools.partial(exchange_kernel, n, hub_dev),
        out_shape=(
            sds((n, tall, wide), BF16), sds((tiles, edge, wide), BF16), sds((tiles, edge, wide), BF16),
            sds(self_weight.shape, BF16), sds(neighbor_weight.shape, BF16),
        ),
        in_specs=[vmem()] * 4 + [smem()] * 2,
        out_specs=(vmem(),) * 5,
        scratch_shapes=[
            pltpu.VMEM((n, tall, half), BF16),
            dma((n,)), dma((n,)), dma((n,)), dma((n,)), dma((2,)), dma((4,)), dma((4,)),
        ],
        compiler_params=params(collective_id=0, has_side_effects=True),
        name="exchange",
    )(
        features.reshape(tiles, edge, half), cotangent.reshape(tiles, edge, half),
        self_weight, neighbor_weight, send_tile, hub_rows,
    )

    feat_index = lax.axis_index("feat").astype(jnp.int32).reshape(1)
    anywhere = pl.BlockSpec(memory_space=pl.ANY)
    slots = tile_values.shape[0]
    parts = math.gcd(slots, 8)
    chunks = tiles // math.gcd(tiles, 4)
    layer, grads, direct, terms = pl.pallas_call(
        functools.partial(local_kernel, hub_dev),
        out_shape=(
            sds((tiles, edge, half), BF16), sds((wide, wide), F32),
            sds((tiles, edge, half), F32), sds((n, tall, half), BF16),
        ),
        in_specs=[smem()] * 4 + [vmem(), anywhere, anywhere] + [vmem()] * 4 + [anywhere, vmem()],
        out_specs=(anywhere, vmem(), anywhere, vmem()),
        scratch_shapes=[
            pltpu.VMEM((tiles, edge, wide), F32),
            pltpu.VMEM((tiles, edge, edge), F32),
            pltpu.VMEM((tiles, half, edge), BF16),
            pltpu.VMEM((n, half, edge), F32),
            pltpu.VMEM((hubs, half), F32),
            pltpu.VMEM((tiles, edge, wide), BF16),
            pltpu.VMEM((tiles, edge, wide), BF16),
            pltpu.VMEM(tile_values.shape, BF16),
            pltpu.VMEM((tiles, edge, half), BF16),
            pltpu.VMEM((tiles, edge, half), F32),
            pltpu.VMEM((2 * wide, wide), BF16),
            pltpu.VMEM((wide, wide), BF16),
            dma((parts,)), dma((2,)), dma((chunks,)), dma((chunks,)),
        ],
        compiler_params=params(),
        name="local_pass",
    )(
        feat_index, tile_row, tile_owner, tile_count, cols, x_all, c_all,
        self_weight, neighbor_weight, ws_other, wn_other, tile_values, hub_panel.T,
    )

    factor = 1.0 / math.sqrt(rows * n)
    back = lax.all_to_all(terms, "dom", split_axis=0, concat_axis=0, tiled=True)
    if wide % (16 * n) == 0:
        part = (n, wide // n, wide)
        self_grad, neighbor_grad = pl.pallas_call(
            functools.partial(reduce_kernel, n, factor),
            out_shape=(sds((half, wide), F32), sds((half, wide), F32)),
            in_specs=[vmem()],
            out_specs=(vmem(),) * 2,
            scratch_shapes=[pltpu.VMEM(part, BF16)] * 3 + [dma((n,))] * 4,
            compiler_params=params(collective_id=1, has_side_effects=True),
            name="reduce_grads",
            cost_estimate=pl.CostEstimate(flops=10**10, bytes_accessed=2**24, transcendentals=0),
        )(grads)
    else:
        total = lax.psum(grads, "dom") * factor
        swapped = jnp.concatenate([total[:, half:], total[:, :half]], axis=1)
        total = jnp.where(feat_index[0] == 0, total, swapped)
        self_grad, neighbor_grad = total[:half], total[half:]

    input_grad = pl.pallas_call(
        functools.partial(finish_kernel, hub_dev),
        out_shape=sds((rows, half), F32),
        in_specs=[smem()] * 2 + [vmem()] * 2,
        out_specs=vmem(),
        compiler_params=params(),
        name="finish",
    )(send_tile, hub_rows, direct.reshape(rows, half), back)
    return layer.reshape(rows, half), self_grad, neighbor_grad, input_grad


def solution(mesh):
    placed = (
        P("dom", "feat"), P("feat", None), P("feat", None), P("dom", None, None), P("dom"), P("dom"),
        P("dom"), P("dom"), P("dom", None), P("dom"), P("dom", "feat"),
    )
    return jax.shard_map(
        shards,
        mesh=mesh,
        in_specs=placed,
        out_specs=(P("dom", "feat"), P("feat", None), P("feat", None), P("dom", "feat")),
        check_vma=False,
    )
```

```python
import functools
import math

import jax
import jax.numpy as jnp
from jax import lax
from jax.experimental import pallas as pl
from jax.experimental.pallas import tpu as pltpu
from jax.sharding import PartitionSpec as P

F32 = jnp.float32
BF16 = jnp.bfloat16
VMEM_BYTES = 58 * 2**20
UNROLL = 8


def vmem():
    return pl.BlockSpec(memory_space=pltpu.VMEM)


def smem():
    return pl.BlockSpec(memory_space=pltpu.SMEM)


def dot(a, b, dims=((1,), (0,))):
    return lax.dot_general(a, b, (dims, ((), ())), preferred_element_type=F32)


def greet(n, me, feat, with_sibling):
    barrier = pltpu.get_barrier_semaphore()

    def hello(d, carry):
        pl.semaphore_signal(
            barrier, inc=1, device_id={"dom": lax.rem(me + d, n)}, device_id_type=pl.DeviceIdType.MESH
        )
        return carry

    lax.fori_loop(1, n, hello, 0)
    if with_sibling:
        pl.semaphore_signal(barrier, inc=1, device_id={"feat": 1 - feat}, device_id_type=pl.DeviceIdType.MESH)


def wait_greetings(count):
    pl.semaphore_wait(pltpu.get_barrier_semaphore(), count)


def mixed(k, n):
    return 1 + lax.rem(k * (n // 2 - 1), n - 1)


def exchange_kernel(
    n, hub_dev, feat_ref, cot_ref, ws_ref, wn_ref, send_ref, hub_ref,
    cols_ref, x_ref, c_ref, wso_ref, wno_ref,
    stage, send_sem, recv_sem, fsend_sem, frecv_sem, loc_sem, esend_sem, erecv_sem,
):
    me = lax.axis_index("dom")
    feat = lax.axis_index("feat")
    edge = feat_ref.shape[1]
    rows = edge * feat_ref.shape[0]
    pad = stage.shape[1] - edge
    half = feat_ref.shape[2]
    greet(n, me, feat, True)

    row_ids = lax.broadcasted_iota(jnp.int32, (edge, half), 0)
    out_ids = lax.broadcasted_iota(jnp.int32, (pad, half), 0)
    hub_block = jnp.zeros((pad, half), F32)
    for h in range(hub_dev):
        r = hub_ref[h]
        tile = feat_ref[r // edge].astype(F32)
        row = jnp.sum(jnp.where(row_ids == r % edge, tile, 0.0), axis=0, keepdims=True)
        hub_block = jnp.where(out_ids == h, row, hub_block)
    hub_block = hub_block.astype(BF16)

    def fill(d, carry):
        stage[d, 0:edge, :] = feat_ref[send_ref[lax.rem(me + d, n)]]
        stage[d, edge:, :] = hub_block
        return carry

    lax.fori_loop(1, n, fill, 0)
    cols_ref[me, 0:edge, 0:half] = feat_ref[send_ref[me]]
    cols_ref[me, edge:, 0:half] = hub_block
    wait_greetings(n)

    def peer_copy(d):
        return pltpu.make_async_remote_copy(
            src_ref=stage.at[d], dst_ref=cols_ref.at[me, :, 0:half],
            send_sem=send_sem.at[d], recv_sem=recv_sem.at[d],
            device_id={"dom": lax.rem(me + d, n)}, device_id_type=pl.DeviceIdType.MESH,
        )

    def forward(q):
        return pltpu.make_async_remote_copy(
            src_ref=cols_ref.at[q, :, 0:half], dst_ref=cols_ref.at[q, :, half:2 * half],
            send_sem=fsend_sem.at[q], recv_sem=frecv_sem.at[q],
            device_id={"feat": 1 - feat}, device_id_type=pl.DeviceIdType.MESH,
        )

    def send(k, carry):
        peer_copy(mixed(k, n)).start()
        return carry

    lax.fori_loop(0, n - 1, send, 0)
    forward(me).start()

    extras = [
        pltpu.make_async_remote_copy(
            src_ref=src, dst_ref=dst, send_sem=esend_sem.at[i], recv_sem=erecv_sem.at[i],
            device_id={"feat": 1 - feat}, device_id_type=pl.DeviceIdType.MESH,
        )
        for i, (src, dst) in enumerate((
            (feat_ref, x_ref.at[:, :, half:2 * half]),
            (cot_ref, c_ref.at[:, :, half:2 * half]),
            (ws_ref, wso_ref),
            (wn_ref, wno_ref),
        ))
    ]
    for copy in extras:
        copy.start()
    locals_ = [
        pltpu.make_async_copy(feat_ref, x_ref.at[:, :, 0:half], loc_sem.at[0]),
        pltpu.make_async_copy(cot_ref, c_ref.at[:, :, 0:half], loc_sem.at[1]),
    ]
    for copy in locals_:
        copy.start()

    def arrive(k, carry):
        d = mixed(k, n)
        peer_copy(d).wait_recv()
        forward(lax.rem(me - d + n, n)).start()
        return carry

    lax.fori_loop(0, n - 1, arrive, 0)
    for copy in locals_:
        copy.wait()
    for copy in extras:
        copy.wait()

    def finish(d, carry):
        peer_copy(d).wait_send()
        return carry

    lax.fori_loop(1, n, finish, 0)

    def finish_forward(q, carry):
        forward(q).wait()
        return carry

    lax.fori_loop(0, n, finish_forward, 0)


def slot_loop(first, last, step):
    full = (last - first) // UNROLL

    def many(i, carry):
        for u in range(UNROLL):
            step(first + i * UNROLL + u)
        return carry

    lax.fori_loop(0, full, many, 0)

    def single(k, carry):
        step(k)
        return carry

    lax.fori_loop(first + full * UNROLL, last, single, 0)


def local_kernel(
    hub_dev, feat_ref, row_ref, owner_ref, count_ref,
    cols_ref, x_hbm, c_hbm, ws_ref, wn_ref, wso_ref, wno_ref, val_hbm, panel_ref,
    out_hbm, grad_ref, direct_hbm, terms_ref,
    acc, sq, slopes_t, terms_t, hub_s, x_ref, c_ref, val_ref, out_ref, direct_ref, w_ahead, w_back,
    val_sem, in_sem, out_sem, direct_sem,
):
    f = feat_ref[0]
    tiles, edge, wide = x_ref.shape
    half = wide // 2
    n = cols_ref.shape[0]
    hubs = panel_ref.shape[0]
    pad = cols_ref.shape[1] - edge
    parts = val_sem.shape[0]
    cap = val_ref.shape[0] // parts
    group = tiles // out_sem.shape[0]
    rows = group * edge
    count = count_ref[0]

    def val_copy(i):
        return pltpu.make_async_copy(
            val_hbm.at[pl.ds(i * cap, cap)], val_ref.at[pl.ds(i * cap, cap)], val_sem.at[i]
        )

    def out_copies(i):
        span = pl.ds(i * group, group)
        return (
            pltpu.make_async_copy(out_ref.at[span], out_hbm.at[span], out_sem.at[i]),
            pltpu.make_async_copy(direct_ref.at[span], direct_hbm.at[span], direct_sem.at[i]),
        )

    for i in range(parts):
        val_copy(i).start()
    x_copy = pltpu.make_async_copy(x_hbm, x_ref, in_sem.at[0])
    c_copy = pltpu.make_async_copy(c_hbm, c_ref, in_sem.at[1])
    x_copy.start()
    c_copy.start()

    def local_order(w):
        return jnp.where(f == 0, w, jnp.concatenate([w[:, half:], w[:, :half]], axis=1))

    ws_own = local_order(ws_ref[...].astype(F32))
    wn_own = local_order(wn_ref[...].astype(F32))
    ws_other = local_order(wso_ref[...].astype(F32))
    wn_other = local_order(wno_ref[...].astype(F32))
    w_ahead[...] = jnp.concatenate([ws_own, ws_other, wn_own, wn_other], axis=0).astype(BF16)
    w_back[...] = jnp.concatenate([ws_own, wn_own], axis=0).T.astype(BF16)

    hub_ids = lax.broadcasted_iota(jnp.int32, (hubs, n * pad), 0)
    place = lax.broadcasted_iota(jnp.int32, (hubs, n * pad), 1)
    pick = (hub_ids // hub_dev == place // pad) & (hub_ids % hub_dev == place % pad)
    hub_rows = cols_ref[:, edge:, :].reshape(n * pad, wide)
    hub_feats = dot(jnp.where(pick, 1.0, 0.0).astype(BF16), hub_rows).astype(BF16)

    def panel_part(i):
        return panel_ref[:, pl.ds(pl.multiple_of(i * rows, rows), rows)]

    def start(i, carry):
        panel = panel_part(i).astype(F32).T
        span = pl.ds(i * group, group)
        acc[span] = dot(panel.astype(BF16), hub_feats).reshape(group, edge, wide)
        squares = panel * panel
        if hubs < edge:
            squares = jnp.concatenate([squares, jnp.zeros((rows, edge - hubs), F32)], axis=1)
        else:
            squares = sum(squares[:, j:j + edge] for j in range(0, hubs, edge))
        sq[span] = squares.reshape(group, edge, edge)
        return carry

    lax.fori_loop(0, tiles // group, start, 0)

    def ahead(k):
        values = val_ref[k]
        row = row_ref[k]
        acc[row] += dot(values, cols_ref[owner_ref[k], 0:edge, :])
        wide_values = values.astype(F32)
        sq[row] += wide_values * wide_values

    def part(i, carry):
        val_copy(i).wait()
        first = i * cap
        slot_loop(first, jnp.clip(count, first, first + cap), ahead)
        return carry

    lax.fori_loop(0, parts, part, 0)

    grad_ref[...] = jnp.zeros_like(grad_ref)
    hub_s[...] = jnp.zeros_like(hub_s)
    ones = jnp.ones((2 * edge, half), BF16)
    x_copy.wait()
    c_copy.wait()

    def dense(i, carry):
        span = pl.ds(i * group, group)
        squares = sq[span].reshape(rows, edge)
        high = squares.astype(BF16)
        low = (squares - high.astype(F32)).astype(BF16)
        inverse = lax.rsqrt(1.0 + dot(jnp.concatenate([high, low], axis=1), ones))
        x = x_ref[span].reshape(rows, wide)
        sums = acc[span].reshape(rows, wide)
        aggregate = (sums * jnp.concatenate([inverse, inverse], axis=1)).astype(BF16)
        preact = dot(jnp.concatenate([x, aggregate], axis=1), w_ahead[...])
        out_ref[span] = jnp.maximum(preact[:, :half], 0.0).astype(BF16).reshape(group, edge, half)
        cotangent = c_ref[span].reshape(rows, wide).astype(F32)
        slopes = jnp.where(preact > 0, cotangent, 0.0).astype(BF16)
        both = dot(slopes, w_back[...])
        direct_ref[span] = both[:, :half].reshape(group, edge, half)
        for copy in out_copies(i):
            copy.start()
        back = (both[:, half:] * inverse).astype(BF16)
        hub_s[...] += dot(panel_part(i), back)
        back_t = back.T
        for g in range(group):
            slopes_t[i * group + g] = back_t[:, g * edge:(g + 1) * edge]
        left = jnp.concatenate([x[:, :half], aggregate[:, :half]], axis=1)
        grad_ref[...] += dot(left, slopes, ((0,), (0,)))
        return carry

    lax.fori_loop(0, tiles // group, dense, 0)

    def clear(o, carry):
        terms_t[o] = jnp.zeros((half, edge), F32)
        return carry

    lax.fori_loop(0, n, clear, 0)

    def behind(k):
        terms_t[owner_ref[k]] += dot(slopes_t[row_ref[k]], val_ref[k])

    slot_loop(0, count, behind)

    hub_terms = hub_s[...]
    high = hub_terms.astype(BF16)
    low = (hub_terms - high.astype(F32)).astype(BF16)
    ids = lax.broadcasted_iota(jnp.int32, (n * pad, hubs), 1)
    spot = lax.broadcasted_iota(jnp.int32, (n * pad, hubs), 0)
    same = ids // hub_dev == spot // pad
    put_high = jnp.where(same & (spot % pad == ids % hub_dev), 1.0, 0.0).astype(BF16)
    put_low = jnp.where(same & (spot % pad == ids % hub_dev + hub_dev), 1.0, 0.0).astype(BF16)
    blocks = dot(put_high, high) + dot(put_low, low)
    terms_ref[:, edge:, :] = blocks.reshape(n, pad, half).astype(BF16)

    def emit(o, carry):
        terms_ref[o, 0:edge, :] = terms_t[o].T.astype(BF16)
        return carry

    lax.fori_loop(0, n, emit, 0)

    def drain(i, carry):
        for copy in out_copies(i):
            copy.wait()
        return carry

    lax.fori_loop(0, tiles // group, drain, 0)


def return_kernel(n, inner, factor, *refs):
    if inner:
        (terms_ref, grad_ref, back_ref, self_ref, neigh_ref,
         send_sem, recv_sem, gstage, gin, hstage, hin, gall, step_send, step_recv) = refs
    else:
        terms_ref, back_ref, send_sem, recv_sem = refs
    me = lax.axis_index("dom")
    feat = lax.axis_index("feat")
    greet(n, me, feat, False)
    if inner:
        gstage[...] = grad_ref[...].astype(BF16).reshape(gstage.shape)
    back_ref[me] = terms_ref[me]
    wait_greetings(n - 1)

    def copy_to(target, src, dst, ssem, rsem):
        return pltpu.make_async_remote_copy(
            src_ref=src, dst_ref=dst, send_sem=ssem, recv_sem=rsem,
            device_id={"dom": target}, device_id_type=pl.DeviceIdType.MESH,
        )

    def term_copy(d):
        q = lax.rem(me + d, n)
        return copy_to(q, terms_ref.at[q], back_ref.at[me], send_sem.at[d], recv_sem.at[d])

    def send_terms(first, last):
        def body(k, carry):
            term_copy(mixed(k, n)).start()
            return carry
        lax.fori_loop(first, last, body, 0)

    batch = -(-(n - 1) // 3)

    def each(fn, size):
        def body(d, carry):
            fn(d)
            return carry
        lax.fori_loop(1, size, body, 0)

    if inner:
        outer = n // inner
        z, i = me // inner, lax.rem(me, inner)

        def plane_copy(d, phase, src, dst):
            j = lax.rem(i + d, inner)
            return copy_to(z * inner + j, src(j), dst, step_send.at[phase, d], step_recv.at[phase, d])

        def line_copy(d, phase, src, dst):
            k = lax.rem(z + d, outer)
            return copy_to(k * inner + i, src(k), dst, step_send.at[phase, d], step_recv.at[phase, d])

        def scatter_plane(d):
            return plane_copy(d, 0, lambda j: gstage.at[j], gin.at[i])

        def scatter_line(d):
            return line_copy(d, 1, lambda k: hstage.at[k], hin.at[z])

        def gather_line(d):
            return line_copy(d, 2, lambda k: gall.at[i, z], gall.at[i, z])

        def gather_plane(d):
            return plane_copy(d, 3, lambda j: gall.at[i], gall.at[i])

        each(lambda d: scatter_plane(d).start(), inner)
        send_terms(0, batch)
        gin[i] = gstage[i]
        each(lambda d: scatter_plane(d).wait_recv(), inner)
        hstage[...] = jnp.sum(gin[...].astype(F32), axis=0).astype(BF16)
        each(lambda d: scatter_line(d).start(), outer)
        send_terms(batch, 2 * batch)
        hin[z] = hstage[z]
        each(lambda d: scatter_line(d).wait_recv(), outer)
        gall[i, z] = jnp.sum(hin[...].astype(F32), axis=0).astype(BF16)
        each(lambda d: gather_line(d).start(), outer)
        send_terms(2 * batch, n - 1)
        each(lambda d: gather_line(d).wait_recv(), outer)
        each(lambda d: gather_plane(d).start(), inner)
    else:
        send_terms(0, n - 1)
    each(lambda d: term_copy(d).wait(), n)
    if inner:
        each(lambda d: scatter_plane(d).wait_send(), inner)
        each(lambda d: scatter_line(d).wait_send(), outer)
        each(lambda d: gather_line(d).wait_send(), outer)
        each(lambda d: gather_plane(d).wait(), inner)
        total = gall[...].astype(F32).reshape(grad_ref.shape) * factor
        half = total.shape[1] // 2
        total = jnp.where(feat == 0, total, jnp.concatenate([total[:, half:], total[:, :half]], axis=1))
        self_ref[...] = total[: self_ref.shape[0]]
        neigh_ref[...] = total[self_ref.shape[0]:]


def finish_kernel(hub_dev, edge, send_ref, hub_ref, direct_hbm, back_ref, out_hbm, total_ref, sem):
    n = back_ref.shape[0]
    load = pltpu.make_async_copy(direct_hbm, total_ref, sem.at[0])
    load.start()
    hub_total = jnp.sum(back_ref[:, edge:, :].astype(F32), axis=0)
    load.wait()

    def add(q, carry):
        rows = pl.ds(pl.multiple_of(send_ref[q] * edge, edge), edge)
        total_ref[rows, :] += back_ref[q, 0:edge, :].astype(F32)
        return carry

    lax.fori_loop(0, n, add, 0)
    for h in range(hub_dev):
        row = hub_total[h:h + 1] + hub_total[hub_dev + h:hub_dev + h + 1]
        total_ref[pl.ds(hub_ref[h], 1), :] += row
    store = pltpu.make_async_copy(total_ref, out_hbm, sem.at[1])
    store.start()
    store.wait()


def shards(
    features, self_weight, neighbor_weight, tile_values, tile_row, tile_owner,
    send_tile, tile_count, hub_panel, hub_rows, cotangent,
):
    rows, half = features.shape
    edge = tile_values.shape[1]
    tiles = rows // edge
    n = lax.axis_size("dom")
    hub_dev = hub_rows.shape[0]
    hubs = hub_panel.shape[1]
    wide = 2 * half
    pad = -(-2 * hub_dev // 16) * 16
    tall = edge + pad
    sds = jax.ShapeDtypeStruct
    dma = pltpu.SemaphoreType.DMA
    anywhere = pl.BlockSpec(memory_space=pl.ANY)
    params = functools.partial(pltpu.CompilerParams, vmem_limit_bytes=VMEM_BYTES)

    cols, x_all, c_all, ws_other, wn_other = pl.pallas_call(
        functools.partial(exchange_kernel, n, hub_dev),
        out_shape=(
            sds((n, tall, wide), BF16), sds((tiles, edge, wide), BF16), sds((tiles, edge, wide), BF16),
            sds(self_weight.shape, BF16), sds(neighbor_weight.shape, BF16),
        ),
        in_specs=[vmem()] * 4 + [smem()] * 2,
        out_specs=(vmem(),) * 5,
        scratch_shapes=[
            pltpu.VMEM((n, tall, half), BF16),
            dma((n,)), dma((n,)), dma((n,)), dma((n,)), dma((2,)), dma((4,)), dma((4,)),
        ],
        compiler_params=params(collective_id=0, has_side_effects=True),
        name="exchange",
    )(
        features.reshape(tiles, edge, half), cotangent.reshape(tiles, edge, half),
        self_weight, neighbor_weight, send_tile, hub_rows,
    )

    feat_index = lax.axis_index("feat").astype(jnp.int32).reshape(1)
    slots = tile_values.shape[0]
    parts = math.gcd(slots, 8)
    chunks = tiles // math.gcd(tiles, 4)
    layer, grads, direct, terms = pl.pallas_call(
        functools.partial(local_kernel, hub_dev),
        out_shape=(
            sds((tiles, edge, half), BF16), sds((wide, wide), F32),
            sds((tiles, edge, half), F32), sds((n, tall, half), BF16),
        ),
        in_specs=[smem()] * 4 + [vmem(), anywhere, anywhere] + [vmem()] * 4 + [anywhere, vmem()],
        out_specs=(anywhere, vmem(), anywhere, vmem()),
        scratch_shapes=[
            pltpu.VMEM((tiles, edge, wide), F32),
            pltpu.VMEM((tiles, edge, edge), F32),
            pltpu.VMEM((tiles, half, edge), BF16),
            pltpu.VMEM((n, half, edge), F32),
            pltpu.VMEM((hubs, half), F32),
            pltpu.VMEM((tiles, edge, wide), BF16),
            pltpu.VMEM((tiles, edge, wide), BF16),
            pltpu.VMEM(tile_values.shape, BF16),
            pltpu.VMEM((tiles, edge, half), BF16),
            pltpu.VMEM((tiles, edge, half), F32),
            pltpu.VMEM((2 * wide, wide), BF16),
            pltpu.VMEM((wide, wide), BF16),
            dma((parts,)), dma((2,)), dma((chunks,)), dma((chunks,)),
        ],
        compiler_params=params(),
        name="local_pass",
    )(
        feat_index, tile_row, tile_owner, tile_count, cols, x_all, c_all,
        self_weight, neighbor_weight, ws_other, wn_other, tile_values, hub_panel.T,
    )

    factor = 1.0 / math.sqrt(rows * n)
    inner = math.isqrt(n)
    if inner * inner != n or wide % (16 * n):
        inner = 0
    back_shape = sds((n, tall, half), BF16)
    if inner:
        line = (inner, wide // n, wide)
        back, self_grad, neighbor_grad = pl.pallas_call(
            functools.partial(return_kernel, n, inner, factor),
            out_shape=(back_shape, sds((half, wide), F32), sds((half, wide), F32)),
            in_specs=[vmem()] * 2,
            out_specs=(vmem(),) * 3,
            scratch_shapes=[
                dma((n,)), dma((n,)),
                pltpu.VMEM((inner,) + line, BF16), pltpu.VMEM((inner,) + line, BF16),
                pltpu.VMEM(line, BF16), pltpu.VMEM(line, BF16),
                pltpu.VMEM((inner,) + line, BF16),
                dma((4, inner)), dma((4, inner)),
            ],
            compiler_params=params(collective_id=1, has_side_effects=True),
            name="send_back",
        )(terms, grads)
    else:
        back = pl.pallas_call(
            functools.partial(return_kernel, n, 0, factor),
            out_shape=back_shape,
            in_specs=[vmem()],
            out_specs=vmem(),
            scratch_shapes=[dma((n,)), dma((n,))],
            compiler_params=params(collective_id=1, has_side_effects=True),
            name="send_back",
        )(terms)
        total = lax.psum(grads, "dom") * factor
        swapped = jnp.concatenate([total[:, half:], total[:, :half]], axis=1)
        total = jnp.where(feat_index[0] == 0, total, swapped)
        self_grad, neighbor_grad = total[:half], total[half:]

    input_grad = pl.pallas_call(
        functools.partial(finish_kernel, hub_dev, edge),
        out_shape=sds((rows, half), F32),
        in_specs=[smem()] * 2 + [anywhere, vmem()],
        out_specs=anywhere,
        scratch_shapes=[pltpu.VMEM((rows, half), F32), dma((2,))],
        compiler_params=params(),
        name="finish",
    )(send_tile, hub_rows, direct.reshape(rows, half), back)
    return layer.reshape(rows, half), self_grad, neighbor_grad, input_grad


def solution(mesh):
    placed = (
        P("dom", "feat"), P("feat", None), P("feat", None), P("dom", None, None), P("dom"), P("dom"),
        P("dom"), P("dom"), P("dom", None), P("dom"), P("dom", "feat"),
    )
    return jax.shard_map(
        shards,
        mesh=mesh,
        in_specs=placed,
        out_specs=(P("dom", "feat"), P("feat", None), P("feat", None), P("dom", "feat")),
        check_vma=False,
    )
```

```python
import functools
import math

import jax
import jax.numpy as jnp
from jax import lax
from jax.experimental import pallas as pl
from jax.experimental.pallas import tpu as pltpu
from jax.sharding import PartitionSpec as P

F32 = jnp.float32
BF16 = jnp.bfloat16
VMEM_BYTES = 58 * 2**20
UNROLL = 8


def vmem():
    return pl.BlockSpec(memory_space=pltpu.VMEM)


def smem():
    return pl.BlockSpec(memory_space=pltpu.SMEM)


def dot(a, b, dims=((1,), (0,))):
    return lax.dot_general(a, b, (dims, ((), ())), preferred_element_type=F32)


def greet(n, me, feat, with_sibling):
    barrier = pltpu.get_barrier_semaphore()

    def hello(d, carry):
        pl.semaphore_signal(
            barrier, inc=1, device_id={"dom": lax.rem(me + d, n)}, device_id_type=pl.DeviceIdType.MESH
        )
        return carry

    lax.fori_loop(1, n, hello, 0)
    if with_sibling:
        pl.semaphore_signal(barrier, inc=1, device_id={"feat": 1 - feat}, device_id_type=pl.DeviceIdType.MESH)


def wait_greetings(count):
    pl.semaphore_wait(pltpu.get_barrier_semaphore(), count)


def mixed(k, n):
    return 1 + lax.rem(k * (n // 2 - 1), n - 1)


def exchange_kernel(
    n, hub_dev, feat_ref, cot_ref, ws_ref, wn_ref, send_ref, hub_ref,
    cols_ref, x_ref, c_ref, wso_ref, wno_ref, xt_ref,
    stage, send_sem, recv_sem, fsend_sem, frecv_sem, loc_sem, esend_sem, erecv_sem,
):
    me = lax.axis_index("dom")
    feat = lax.axis_index("feat")
    edge = feat_ref.shape[1]
    rows = edge * feat_ref.shape[0]
    pad = stage.shape[1] - edge
    half = feat_ref.shape[2]
    greet(n, me, feat, True)
    wait_greetings(n)

    row_ids = lax.broadcasted_iota(jnp.int32, (edge, half), 0)
    out_ids = lax.broadcasted_iota(jnp.int32, (pad, half), 0)
    hub_block = jnp.zeros((pad, half), F32)
    for h in range(hub_dev):
        r = hub_ref[h]
        tile = feat_ref[r // edge].astype(F32)
        row = jnp.sum(jnp.where(row_ids == r % edge, tile, 0.0), axis=0, keepdims=True)
        hub_block = jnp.where(out_ids == h, row, hub_block)
    hub_block = hub_block.astype(BF16)

    def peer_copy(d):
        return pltpu.make_async_remote_copy(
            src_ref=stage.at[d], dst_ref=cols_ref.at[me, :, 0:half],
            send_sem=send_sem.at[d], recv_sem=recv_sem.at[d],
            device_id={"dom": lax.rem(me + d, n)}, device_id_type=pl.DeviceIdType.MESH,
        )

    def forward(q):
        return pltpu.make_async_remote_copy(
            src_ref=cols_ref.at[q, :, 0:half], dst_ref=cols_ref.at[q, :, half:2 * half],
            send_sem=fsend_sem.at[q], recv_sem=frecv_sem.at[q],
            device_id={"feat": 1 - feat}, device_id_type=pl.DeviceIdType.MESH,
        )

    def send(d, carry):
        q = lax.rem(me + d, n)
        stage[d, 0:edge, :] = feat_ref[send_ref[q]]
        stage[d, edge:, :] = hub_block
        peer_copy(d).start()
        return carry

    lax.fori_loop(1, n, send, 0)
    cols_ref[me, 0:edge, 0:half] = feat_ref[send_ref[me]]
    cols_ref[me, edge:, 0:half] = hub_block
    forward(me).start()

    extras = [
        pltpu.make_async_remote_copy(
            src_ref=src, dst_ref=dst, send_sem=esend_sem.at[i], recv_sem=erecv_sem.at[i],
            device_id={"feat": 1 - feat}, device_id_type=pl.DeviceIdType.MESH,
        )
        for i, (src, dst) in enumerate((
            (feat_ref, x_ref.at[:, :, half:2 * half]),
            (cot_ref, c_ref.at[:, :, half:2 * half]),
            (ws_ref, wso_ref),
            (wn_ref, wno_ref),
        ))
    ]
    for copy in extras:
        copy.start()
    locals_ = [
        pltpu.make_async_copy(feat_ref, x_ref.at[:, :, 0:half], loc_sem.at[0]),
        pltpu.make_async_copy(cot_ref, c_ref.at[:, :, 0:half], loc_sem.at[1]),
    ]
    for copy in locals_:
        copy.start()

    for t in range(feat_ref.shape[0]):
        xt_ref[:, t * edge:(t + 1) * edge] = feat_ref[t].T

    def arrive(d, carry):
        peer_copy(d).wait_recv()
        forward(lax.rem(me - d + n, n)).start()
        return carry

    lax.fori_loop(1, n, arrive, 0)
    for copy in locals_:
        copy.wait()
    for copy in extras:
        copy.wait()

    def finish(d, carry):
        peer_copy(d).wait_send()
        return carry

    lax.fori_loop(1, n, finish, 0)

    def finish_forward(q, carry):
        forward(q).wait()
        return carry

    lax.fori_loop(0, n, finish_forward, 0)


def slot_loop(first, last, step):
    full = (last - first) // UNROLL

    def many(i, carry):
        for u in range(UNROLL):
            step(first + i * UNROLL + u)
        return carry

    lax.fori_loop(0, full, many, 0)

    def single(k, carry):
        step(k)
        return carry

    lax.fori_loop(first + full * UNROLL, last, single, 0)


def local_kernel(
    hub_dev, feat_ref, row_ref, owner_ref, count_ref,
    cols_ref, x_hbm, c_hbm, ws_ref, wn_ref, wso_ref, wno_ref, val_hbm, panel_ref, xt_hbm,
    out_hbm, grad_ref, direct_hbm, terms_ref,
    acc, sq, slopes_t, terms_t, hub_s, x_ref, c_ref, xt_ref, val_ref, out_ref, direct_ref, w_ahead, w_back,
    val_sem, in_sem, out_sem, direct_sem,
):
    f = feat_ref[0]
    tiles, edge, wide = x_ref.shape
    half = wide // 2
    n = cols_ref.shape[0]
    hubs = panel_ref.shape[0]
    pad = cols_ref.shape[1] - edge
    parts = val_sem.shape[0]
    cap = val_ref.shape[0] // parts
    group = tiles // out_sem.shape[0]
    rows = group * edge
    count = count_ref[0]

    def val_copy(i):
        return pltpu.make_async_copy(
            val_hbm.at[pl.ds(i * cap, cap)], val_ref.at[pl.ds(i * cap, cap)], val_sem.at[i]
        )

    def out_copies(i):
        span = pl.ds(i * group, group)
        return (
            pltpu.make_async_copy(out_ref.at[span], out_hbm.at[span], out_sem.at[i]),
            pltpu.make_async_copy(direct_ref.at[span], direct_hbm.at[span], direct_sem.at[i]),
        )

    for i in range(parts):
        val_copy(i).start()
    x_copy = pltpu.make_async_copy(x_hbm, x_ref, in_sem.at[0])
    c_copy = pltpu.make_async_copy(c_hbm, c_ref, in_sem.at[1])
    xt_copy = pltpu.make_async_copy(xt_hbm, xt_ref, in_sem.at[2])
    x_copy.start()
    c_copy.start()
    xt_copy.start()

    def local_order(w):
        return jnp.where(f == 0, w, jnp.concatenate([w[:, half:], w[:, :half]], axis=1))

    ws_own = local_order(ws_ref[...].astype(F32))
    wn_own = local_order(wn_ref[...].astype(F32))
    ws_other = local_order(wso_ref[...].astype(F32))
    wn_other = local_order(wno_ref[...].astype(F32))
    w_ahead[...] = jnp.concatenate([ws_own, ws_other, wn_own, wn_other], axis=0).astype(BF16)
    w_back[...] = jnp.concatenate([ws_own, wn_own], axis=0).T.astype(BF16)

    hub_ids = lax.broadcasted_iota(jnp.int32, (hubs, n * pad), 0)
    place = lax.broadcasted_iota(jnp.int32, (hubs, n * pad), 1)
    pick = (hub_ids // hub_dev == place // pad) & (hub_ids % hub_dev == place % pad)
    hub_rows = cols_ref[:, edge:, :].reshape(n * pad, wide)
    hub_feats = dot(jnp.where(pick, 1.0, 0.0).astype(BF16), hub_rows).astype(BF16)

    def panel_part(i):
        return panel_ref[:, pl.ds(pl.multiple_of(i * rows, rows), rows)]

    def start(i, carry):
        panel = panel_part(i).astype(F32).T
        span = pl.ds(i * group, group)
        acc[span] = dot(panel.astype(BF16), hub_feats).reshape(group, edge, wide)
        squares = panel * panel
        if hubs < edge:
            squares = jnp.concatenate([squares, jnp.zeros((rows, edge - hubs), F32)], axis=1)
        else:
            squares = sum(squares[:, j:j + edge] for j in range(0, hubs, edge))
        sq[span] = squares.reshape(group, edge, edge)
        return carry

    lax.fori_loop(0, tiles // group, start, 0)

    def ahead(k):
        values = val_ref[k]
        row = row_ref[k]
        acc[row] += dot(values, cols_ref[owner_ref[k], 0:edge, :])
        wide_values = values.astype(F32)
        sq[row] += wide_values * wide_values

    def part(i, carry):
        val_copy(i).wait()
        first = i * cap
        slot_loop(first, jnp.clip(count, first, first + cap), ahead)
        return carry

    lax.fori_loop(0, parts, part, 0)

    grad_ref[...] = jnp.zeros_like(grad_ref)
    hub_s[...] = jnp.zeros_like(hub_s)
    ones = jnp.ones((2 * edge, half), BF16)
    x_copy.wait()
    c_copy.wait()
    xt_copy.wait()

    def dense(i, carry):
        span = pl.ds(i * group, group)
        squares = sq[span].reshape(rows, edge)
        high = squares.astype(BF16)
        low = (squares - high.astype(F32)).astype(BF16)
        inverse = lax.rsqrt(1.0 + dot(jnp.concatenate([high, low], axis=1), ones))
        x = x_ref[span].reshape(rows, wide)
        sums = acc[span].reshape(rows, wide)
        aggregate = (sums * jnp.concatenate([inverse, inverse], axis=1)).astype(BF16)
        preact = dot(jnp.concatenate([x, aggregate], axis=1), w_ahead[...])
        out_ref[span] = jnp.maximum(preact[:, :half], 0.0).astype(BF16).reshape(group, edge, half)
        cotangent = c_ref[span].reshape(rows, wide).astype(F32)
        slopes = jnp.where(preact > 0, cotangent, 0.0).astype(BF16)
        both = dot(slopes, w_back[...])
        direct_ref[span] = both[:, :half].reshape(group, edge, half)
        for copy in out_copies(i):
            copy.start()
        back = (both[:, half:] * inverse).astype(BF16)
        hub_s[...] += dot(panel_part(i), back)
        back_t = back.T
        for g in range(group):
            slopes_t[i * group + g] = back_t[:, g * edge:(g + 1) * edge]
        x_turned = xt_ref[:, pl.ds(pl.multiple_of(i * rows, rows), rows)]
        grad_ref[0:half] += dot(x_turned, slopes)
        grad_ref[half:] += dot(aggregate[:, :half], slopes, ((0,), (0,)))
        return carry

    lax.fori_loop(0, tiles // group, dense, 0)

    def clear(o, carry):
        terms_t[o] = jnp.zeros((half, edge), F32)
        return carry

    lax.fori_loop(0, n, clear, 0)

    def behind(k):
        terms_t[owner_ref[k]] += dot(slopes_t[row_ref[k]], val_ref[k])

    slot_loop(0, count, behind)

    hub_terms = hub_s[...]
    high = hub_terms.astype(BF16)
    low = (hub_terms - high.astype(F32)).astype(BF16)
    ids = lax.broadcasted_iota(jnp.int32, (n * pad, hubs), 1)
    spot = lax.broadcasted_iota(jnp.int32, (n * pad, hubs), 0)
    same = ids // hub_dev == spot // pad
    put_high = jnp.where(same & (spot % pad == ids % hub_dev), 1.0, 0.0).astype(BF16)
    put_low = jnp.where(same & (spot % pad == ids % hub_dev + hub_dev), 1.0, 0.0).astype(BF16)
    blocks = dot(put_high, high) + dot(put_low, low)
    terms_ref[:, edge:, :] = blocks.reshape(n, pad, half).astype(BF16)

    def emit(o, carry):
        terms_ref[o, 0:edge, :] = terms_t[o].astype(BF16).T
        return carry

    lax.fori_loop(0, n, emit, 0)

    def drain(i, carry):
        for copy in out_copies(i):
            copy.wait()
        return carry

    lax.fori_loop(0, tiles // group, drain, 0)


def return_kernel(n, inner, *refs):
    if inner:
        (terms_ref, grad_ref, back_ref, gall,
         send_sem, recv_sem, gstage, gin, hstage, hin, step_send, step_recv) = refs
    else:
        terms_ref, back_ref, send_sem, recv_sem = refs
    me = lax.axis_index("dom")
    feat = lax.axis_index("feat")
    greet(n, me, feat, False)
    if inner:
        gstage[...] = grad_ref[...].astype(BF16).reshape(gstage.shape)
    back_ref[me] = terms_ref[me]
    wait_greetings(n - 1)

    def copy_to(target, src, dst, ssem, rsem):
        return pltpu.make_async_remote_copy(
            src_ref=src, dst_ref=dst, send_sem=ssem, recv_sem=rsem,
            device_id={"dom": target}, device_id_type=pl.DeviceIdType.MESH,
        )

    def term_copy(d):
        q = lax.rem(me + d, n)
        return copy_to(q, terms_ref.at[q], back_ref.at[me], send_sem.at[d], recv_sem.at[d])

    def send_terms(first, last):
        def body(k, carry):
            term_copy(mixed(k, n)).start()
            return carry
        lax.fori_loop(first, last, body, 0)

    batch = -(-(n - 1) // 3)

    def each(fn, size):
        def body(d, carry):
            fn(d)
            return carry
        lax.fori_loop(1, size, body, 0)

    if inner:
        outer = n // inner
        z, i = me // inner, lax.rem(me, inner)

        def plane_copy(d, phase, src, dst):
            j = lax.rem(i + d, inner)
            return copy_to(z * inner + j, src(j), dst, step_send.at[phase, d], step_recv.at[phase, d])

        def line_copy(d, phase, src, dst):
            k = lax.rem(z + d, outer)
            return copy_to(k * inner + i, src(k), dst, step_send.at[phase, d], step_recv.at[phase, d])

        def scatter_plane(d):
            return plane_copy(d, 0, lambda j: gstage.at[j], gin.at[i])

        def scatter_line(d):
            return line_copy(d, 1, lambda k: hstage.at[k], hin.at[z])

        def gather_line(d):
            return line_copy(d, 2, lambda k: gall.at[i, z], gall.at[i, z])

        def gather_plane(d):
            return plane_copy(d, 3, lambda j: gall.at[i], gall.at[i])

        each(lambda d: scatter_plane(d).start(), inner)
        send_terms(0, batch)
        gin[i] = gstage[i]
        each(lambda d: scatter_plane(d).wait_recv(), inner)
        hstage[...] = jnp.sum(gin[...].astype(F32), axis=0).astype(BF16)
        each(lambda d: scatter_line(d).start(), outer)
        send_terms(batch, 2 * batch)
        hin[z] = hstage[z]
        each(lambda d: scatter_line(d).wait_recv(), outer)
        gall[i, z] = jnp.sum(hin[...].astype(F32), axis=0).astype(BF16)
        each(lambda d: gather_line(d).start(), outer)
        send_terms(2 * batch, n - 1)
        each(lambda d: gather_line(d).wait_recv(), outer)
        each(lambda d: gather_plane(d).start(), inner)
    else:
        send_terms(0, n - 1)
    each(lambda d: term_copy(d).wait(), n)
    if inner:
        each(lambda d: scatter_plane(d).wait_send(), inner)
        each(lambda d: scatter_line(d).wait_send(), outer)
        each(lambda d: gather_line(d).wait_send(), outer)
        each(lambda d: gather_plane(d).wait(), inner)


def finish_kernel(
    hub_dev, edge, factor, send_ref, hub_ref, feat_ref, direct_ref, back_ref, sum_ref,
    out_ref, self_ref, neigh_ref,
):
    n = back_ref.shape[0]
    half = out_ref.shape[1]
    out_ref[...] = direct_ref[...]

    def add(q, carry):
        rows = pl.ds(pl.multiple_of(send_ref[q] * edge, edge), edge)
        out_ref[rows, :] += back_ref[q, 0:edge, :].astype(F32)
        return carry

    lax.fori_loop(0, n, add, 0)
    hub_total = jnp.sum(back_ref[:, edge:, :].astype(F32), axis=0)
    for h in range(hub_dev):
        row = hub_total[h:h + 1] + hub_total[hub_dev + h:hub_dev + h + 1]
        out_ref[pl.ds(hub_ref[h], 1), :] += row
    total = sum_ref[...].astype(F32) * factor
    swapped = jnp.concatenate([total[:, half:], total[:, :half]], axis=1)
    total = jnp.where(feat_ref[0] == 0, total, swapped)
    self_ref[...] = total[:half]
    neigh_ref[...] = total[half:]


def shards(
    features, self_weight, neighbor_weight, tile_values, tile_row, tile_owner,
    send_tile, tile_count, hub_panel, hub_rows, cotangent,
):
    rows, half = features.shape
    edge = tile_values.shape[1]
    tiles = rows // edge
    n = lax.axis_size("dom")
    hub_dev = hub_rows.shape[0]
    hubs = hub_panel.shape[1]
    wide = 2 * half
    pad = -(-2 * hub_dev // 16) * 16
    tall = edge + pad
    sds = jax.ShapeDtypeStruct
    dma = pltpu.SemaphoreType.DMA
    anywhere = pl.BlockSpec(memory_space=pl.ANY)
    params = functools.partial(pltpu.CompilerParams, vmem_limit_bytes=VMEM_BYTES)

    cols, x_all, c_all, ws_other, wn_other, x_turned = pl.pallas_call(
        functools.partial(exchange_kernel, n, hub_dev),
        out_shape=(
            sds((n, tall, wide), BF16), sds((tiles, edge, wide), BF16), sds((tiles, edge, wide), BF16),
            sds(self_weight.shape, BF16), sds(neighbor_weight.shape, BF16), sds((half, rows), BF16),
        ),
        in_specs=[vmem()] * 4 + [smem()] * 2,
        out_specs=(vmem(),) * 6,
        scratch_shapes=[
            pltpu.VMEM((n, tall, half), BF16),
            dma((n,)), dma((n,)), dma((n,)), dma((n,)), dma((2,)), dma((4,)), dma((4,)),
        ],
        compiler_params=params(collective_id=0, has_side_effects=True),
        name="exchange",
    )(
        features.reshape(tiles, edge, half), cotangent.reshape(tiles, edge, half),
        self_weight, neighbor_weight, send_tile, hub_rows,
    )

    feat_index = lax.axis_index("feat").astype(jnp.int32).reshape(1)
    slots = tile_values.shape[0]
    parts = math.gcd(slots, 8)
    chunks = tiles // math.gcd(tiles, 4)
    layer, grads, direct, terms = pl.pallas_call(
        functools.partial(local_kernel, hub_dev),
        out_shape=(
            sds((tiles, edge, half), BF16), sds((wide, wide), F32),
            sds((tiles, edge, half), F32), sds((n, tall, half), BF16),
        ),
        in_specs=[smem()] * 4 + [vmem(), anywhere, anywhere] + [vmem()] * 4 + [anywhere, vmem(), anywhere],
        out_specs=(anywhere, vmem(), anywhere, vmem()),
        scratch_shapes=[
            pltpu.VMEM((tiles, edge, wide), F32),
            pltpu.VMEM((tiles, edge, edge), F32),
            pltpu.VMEM((tiles, half, edge), BF16),
            pltpu.VMEM((n, half, edge), F32),
            pltpu.VMEM((hubs, half), F32),
            pltpu.VMEM((tiles, edge, wide), BF16),
            pltpu.VMEM((tiles, edge, wide), BF16),
            pltpu.VMEM((half, rows), BF16),
            pltpu.VMEM(tile_values.shape, BF16),
            pltpu.VMEM((tiles, edge, half), BF16),
            pltpu.VMEM((tiles, edge, half), F32),
            pltpu.VMEM((2 * wide, wide), BF16),
            pltpu.VMEM((wide, wide), BF16),
            dma((parts,)), dma((3,)), dma((chunks,)), dma((chunks,)),
        ],
        compiler_params=params(),
        name="local_pass",
    )(
        feat_index, tile_row, tile_owner, tile_count, cols, x_all, c_all,
        self_weight, neighbor_weight, ws_other, wn_other, tile_values, hub_panel.T,
        x_turned,
    )

    factor = 1.0 / math.sqrt(rows * n)
    inner = math.isqrt(n)
    if inner * inner != n or wide % (16 * n):
        inner = 0
    back_shape = sds((n, tall, half), BF16)
    if inner:
        line = (inner, wide // n, wide)
        back, sums = pl.pallas_call(
            functools.partial(return_kernel, n, inner),
            out_shape=(back_shape, sds((inner,) + line, BF16)),
            in_specs=[vmem()] * 2,
            out_specs=(vmem(),) * 2,
            scratch_shapes=[
                dma((n,)), dma((n,)),
                pltpu.VMEM((inner,) + line, BF16), pltpu.VMEM((inner,) + line, BF16),
                pltpu.VMEM(line, BF16), pltpu.VMEM(line, BF16),
                dma((4, inner)), dma((4, inner)),
            ],
            compiler_params=params(collective_id=1, has_side_effects=True),
            name="send_back",
        )(terms, grads)
    else:
        back = pl.pallas_call(
            functools.partial(return_kernel, n, 0),
            out_shape=back_shape,
            in_specs=[vmem()],
            out_specs=vmem(),
            scratch_shapes=[dma((n,)), dma((n,))],
            compiler_params=params(collective_id=1, has_side_effects=True),
            name="send_back",
        )(terms)
        sums = lax.psum(grads, "dom")

    input_grad, self_grad, neighbor_grad = pl.pallas_call(
        functools.partial(finish_kernel, hub_dev, edge, factor),
        out_shape=(sds((rows, half), F32), sds((half, wide), F32), sds((half, wide), F32)),
        in_specs=[smem()] * 3 + [vmem()] * 3,
        out_specs=(vmem(),) * 3,
        compiler_params=params(),
        name="finish",
    )(send_tile, hub_rows, feat_index, direct.reshape(rows, half), back, sums.reshape(wide, wide))
    return layer.reshape(rows, half), self_grad, neighbor_grad, input_grad


def solution(mesh):
    placed = (
        P("dom", "feat"), P("feat", None), P("feat", None), P("dom", None, None), P("dom"), P("dom"),
        P("dom"), P("dom"), P("dom", None), P("dom"), P("dom", "feat"),
    )
    return jax.shard_map(
        shards,
        mesh=mesh,
        in_specs=placed,
        out_specs=(P("dom", "feat"), P("feat", None), P("feat", None), P("dom", "feat")),
        check_vma=False,
    )
```

```python
import functools
import math

import jax
import jax.numpy as jnp
from jax import lax
from jax.experimental import pallas as pl
from jax.experimental.pallas import tpu as pltpu
from jax.sharding import PartitionSpec as P

F32 = jnp.float32
BF16 = jnp.bfloat16
VMEM_BYTES = 58 * 2**20
UNROLL = 10


def vmem():
    return pl.BlockSpec(memory_space=pltpu.VMEM)


def smem():
    return pl.BlockSpec(memory_space=pltpu.SMEM)


def dot(a, b, dims=((1,), (0,))):
    return lax.dot_general(a, b, (dims, ((), ())), preferred_element_type=F32)


def greet(n, me, feat, with_sibling):
    barrier = pltpu.get_barrier_semaphore()

    def hello(d, carry):
        pl.semaphore_signal(
            barrier, inc=1, device_id={"dom": lax.rem(me + d, n)}, device_id_type=pl.DeviceIdType.MESH
        )
        return carry

    lax.fori_loop(1, n, hello, 0)
    if with_sibling:
        pl.semaphore_signal(barrier, inc=1, device_id={"feat": 1 - feat}, device_id_type=pl.DeviceIdType.MESH)


def wait_greetings(count):
    pl.semaphore_wait(pltpu.get_barrier_semaphore(), count)


def mixed(k, n):
    return 1 + lax.rem(k * (n // 2 - 1), n - 1)


def exchange_kernel(
    n, hub_dev, feat_ref, cot_ref, ws_ref, wn_ref, send_ref, hub_ref,
    cols_ref, x_ref, c_ref, wso_ref, wno_ref, xt_ref,
    stage, send_sem, recv_sem, fsend_sem, frecv_sem, loc_sem, esend_sem, erecv_sem,
):
    me = lax.axis_index("dom")
    feat = lax.axis_index("feat")
    edge = feat_ref.shape[1]
    rows = edge * feat_ref.shape[0]
    pad = stage.shape[1] - edge
    half = feat_ref.shape[2]
    greet(n, me, feat, True)
    wait_greetings(n)

    row_ids = lax.broadcasted_iota(jnp.int32, (edge, half), 0)
    out_ids = lax.broadcasted_iota(jnp.int32, (pad, half), 0)
    hub_block = jnp.zeros((pad, half), F32)
    for h in range(hub_dev):
        r = hub_ref[h]
        tile = feat_ref[r // edge].astype(F32)
        row = jnp.sum(jnp.where(row_ids == r % edge, tile, 0.0), axis=0, keepdims=True)
        hub_block = jnp.where(out_ids == h, row, hub_block)
    hub_block = hub_block.astype(BF16)

    def peer_copy(d):
        return pltpu.make_async_remote_copy(
            src_ref=stage.at[d], dst_ref=cols_ref.at[me, :, 0:half],
            send_sem=send_sem.at[d], recv_sem=recv_sem.at[d],
            device_id={"dom": lax.rem(me + d, n)}, device_id_type=pl.DeviceIdType.MESH,
        )

    def forward(q):
        return pltpu.make_async_remote_copy(
            src_ref=cols_ref.at[q, :, 0:half], dst_ref=cols_ref.at[q, :, half:2 * half],
            send_sem=fsend_sem.at[q], recv_sem=frecv_sem.at[q],
            device_id={"feat": 1 - feat}, device_id_type=pl.DeviceIdType.MESH,
        )

    def send(d, carry):
        q = lax.rem(me + d, n)
        stage[d, 0:edge, :] = feat_ref[send_ref[q]]
        stage[d, edge:, :] = hub_block
        peer_copy(d).start()
        return carry

    lax.fori_loop(1, n, send, 0)
    cols_ref[me, 0:edge, 0:half] = feat_ref[send_ref[me]]
    cols_ref[me, edge:, 0:half] = hub_block
    forward(me).start()

    extras = [
        pltpu.make_async_remote_copy(
            src_ref=src, dst_ref=dst, send_sem=esend_sem.at[i], recv_sem=erecv_sem.at[i],
            device_id={"feat": 1 - feat}, device_id_type=pl.DeviceIdType.MESH,
        )
        for i, (src, dst) in enumerate((
            (feat_ref, x_ref.at[:, :, half:2 * half]),
            (cot_ref, c_ref.at[:, :, half:2 * half]),
            (ws_ref, wso_ref),
            (wn_ref, wno_ref),
        ))
    ]
    for copy in extras:
        copy.start()
    locals_ = [
        pltpu.make_async_copy(feat_ref, x_ref.at[:, :, 0:half], loc_sem.at[0]),
        pltpu.make_async_copy(cot_ref, c_ref.at[:, :, 0:half], loc_sem.at[1]),
    ]
    for copy in locals_:
        copy.start()

    for t in range(feat_ref.shape[0]):
        xt_ref[:, t * edge:(t + 1) * edge] = feat_ref[t].T

    def arrive(d, carry):
        peer_copy(d).wait_recv()
        forward(lax.rem(me - d + n, n)).start()
        return carry

    lax.fori_loop(1, n, arrive, 0)
    for copy in locals_:
        copy.wait()
    for copy in extras:
        copy.wait()

    def finish(d, carry):
        peer_copy(d).wait_send()
        return carry

    lax.fori_loop(1, n, finish, 0)

    def finish_forward(q, carry):
        forward(q).wait()
        return carry

    lax.fori_loop(0, n, finish_forward, 0)


def slot_loop(first, last, step):
    full = (last - first) // UNROLL

    def many(i, carry):
        for u in range(UNROLL):
            step(first + i * UNROLL + u)
        return carry

    lax.fori_loop(0, full, many, 0)

    def single(k, carry):
        step(k)
        return carry

    lax.fori_loop(first + full * UNROLL, last, single, 0)


def local_kernel(
    hub_dev, feat_ref, row_ref, owner_ref, count_ref,
    cols_ref, x_hbm, c_hbm, ws_ref, wn_ref, wso_ref, wno_ref, val_hbm, panel_ref, xt_hbm,
    out_hbm, grad_ref, direct_hbm, terms_ref,
    acc, sq, slopes_t, terms_t, hub_s, x_ref, c_ref, xt_ref, val_ref, out_ref, direct_ref, w_ahead, w_back,
    val_sem, in_sem, out_sem, direct_sem,
):
    f = feat_ref[0]
    tiles, edge, wide = x_ref.shape
    half = wide // 2
    n = cols_ref.shape[0]
    hubs = panel_ref.shape[0]
    pad = cols_ref.shape[1] - edge
    parts = val_sem.shape[0]
    cap = val_ref.shape[0] // parts
    group = tiles // out_sem.shape[0]
    rows = group * edge
    count = count_ref[0]

    def val_copy(i):
        return pltpu.make_async_copy(
            val_hbm.at[pl.ds(i * cap, cap)], val_ref.at[pl.ds(i * cap, cap)], val_sem.at[i]
        )

    def out_copies(i):
        span = pl.ds(i * group, group)
        return (
            pltpu.make_async_copy(out_ref.at[span], out_hbm.at[span], out_sem.at[i]),
            pltpu.make_async_copy(direct_ref.at[span], direct_hbm.at[span], direct_sem.at[i]),
        )

    for i in range(parts):
        val_copy(i).start()
    x_copy = pltpu.make_async_copy(x_hbm, x_ref, in_sem.at[0])
    c_copy = pltpu.make_async_copy(c_hbm, c_ref, in_sem.at[1])
    xt_copy = pltpu.make_async_copy(xt_hbm, xt_ref, in_sem.at[2])
    x_copy.start()
    c_copy.start()
    xt_copy.start()

    def local_order(w):
        return jnp.where(f == 0, w, jnp.concatenate([w[:, half:], w[:, :half]], axis=1))

    ws_own = local_order(ws_ref[...].astype(F32))
    wn_own = local_order(wn_ref[...].astype(F32))
    ws_other = local_order(wso_ref[...].astype(F32))
    wn_other = local_order(wno_ref[...].astype(F32))
    w_ahead[...] = jnp.concatenate([ws_own, ws_other, wn_own, wn_other], axis=0).astype(BF16)
    w_back[...] = jnp.concatenate([ws_own, wn_own], axis=0).T.astype(BF16)

    hub_ids = lax.broadcasted_iota(jnp.int32, (hubs, n * pad), 0)
    place = lax.broadcasted_iota(jnp.int32, (hubs, n * pad), 1)
    pick = (hub_ids // hub_dev == place // pad) & (hub_ids % hub_dev == place % pad)
    hub_rows = cols_ref[:, edge:, :].reshape(n * pad, wide)
    hub_feats = dot(jnp.where(pick, 1.0, 0.0).astype(BF16), hub_rows).astype(BF16)

    def panel_part(i):
        return panel_ref[:, pl.ds(pl.multiple_of(i * rows, rows), rows)]

    def start(i, carry):
        panel = panel_part(i).astype(F32).T
        span = pl.ds(i * group, group)
        acc[span] = dot(panel.astype(BF16), hub_feats).reshape(group, edge, wide)
        squares = panel * panel
        if hubs < edge:
            squares = jnp.concatenate([squares, jnp.zeros((rows, edge - hubs), F32)], axis=1)
        else:
            squares = sum(squares[:, j:j + edge] for j in range(0, hubs, edge))
        sq[span] = squares.reshape(group, edge, edge)
        return carry

    lax.fori_loop(0, tiles // group, start, 0)

    def ahead(k):
        values = val_ref[k]
        row = row_ref[k]
        acc[row] += dot(values, cols_ref[owner_ref[k], 0:edge, :])
        wide_values = values.astype(F32)
        sq[row] += wide_values * wide_values

    def part(i, carry):
        val_copy(i).wait()
        first = i * cap
        slot_loop(first, jnp.clip(count, first, first + cap), ahead)
        return carry

    lax.fori_loop(0, parts, part, 0)

    grad_ref[...] = jnp.zeros_like(grad_ref)
    hub_s[...] = jnp.zeros_like(hub_s)
    ones = jnp.ones((2 * edge, half), BF16)
    x_copy.wait()
    c_copy.wait()
    xt_copy.wait()

    def dense(i, carry):
        span = pl.ds(i * group, group)
        squares = sq[span].reshape(rows, edge)
        high = squares.astype(BF16)
        low = (squares - high.astype(F32)).astype(BF16)
        inverse = lax.rsqrt(1.0 + dot(jnp.concatenate([high, low], axis=1), ones))
        x = x_ref[span].reshape(rows, wide)
        sums = acc[span].reshape(rows, wide)
        aggregate = (sums * jnp.concatenate([inverse, inverse], axis=1)).astype(BF16)
        preact = dot(jnp.concatenate([x, aggregate], axis=1), w_ahead[...])
        out_ref[span] = jnp.maximum(preact[:, :half], 0.0).astype(BF16).reshape(group, edge, half)
        cotangent = c_ref[span].reshape(rows, wide).astype(F32)
        slopes = jnp.where(preact > 0, cotangent, 0.0).astype(BF16)
        both = dot(slopes, w_back[...])
        direct_ref[span] = both[:, :half].reshape(group, edge, half)
        for copy in out_copies(i):
            copy.start()
        back = (both[:, half:] * inverse).astype(BF16)
        hub_s[...] += dot(panel_part(i), back)
        back_t = back.T
        for g in range(group):
            slopes_t[i * group + g] = back_t[:, g * edge:(g + 1) * edge]
        x_turned = xt_ref[:, pl.ds(pl.multiple_of(i * rows, rows), rows)]
        grad_ref[0:half] += dot(x_turned, slopes)
        grad_ref[half:] += dot(aggregate[:, :half], slopes, ((0,), (0,)))
        return carry

    lax.fori_loop(0, tiles // group, dense, 0)

    def clear(o, carry):
        terms_t[o] = jnp.zeros((half, edge), F32)
        return carry

    lax.fori_loop(0, n, clear, 0)

    def behind(k):
        terms_t[owner_ref[k]] += dot(slopes_t[row_ref[k]], val_ref[k])

    slot_loop(0, count, behind)

    hub_terms = hub_s[...]
    high = hub_terms.astype(BF16)
    low = (hub_terms - high.astype(F32)).astype(BF16)
    ids = lax.broadcasted_iota(jnp.int32, (n * pad, hubs), 1)
    spot = lax.broadcasted_iota(jnp.int32, (n * pad, hubs), 0)
    same = ids // hub_dev == spot // pad
    put_high = jnp.where(same & (spot % pad == ids % hub_dev), 1.0, 0.0).astype(BF16)
    put_low = jnp.where(same & (spot % pad == ids % hub_dev + hub_dev), 1.0, 0.0).astype(BF16)
    blocks = dot(put_high, high) + dot(put_low, low)
    terms_ref[:, edge:, :] = blocks.reshape(n, pad, half).astype(BF16)

    def emit(o, carry):
        terms_ref[o, 0:edge, :] = terms_t[o].astype(BF16).T
        return carry

    lax.fori_loop(0, n, emit, 0)

    def drain(i, carry):
        for copy in out_copies(i):
            copy.wait()
        return carry

    lax.fori_loop(0, tiles // group, drain, 0)


def return_kernel(n, inner, *refs):
    if inner:
        (terms_ref, grad_ref, back_ref, gall,
         send_sem, recv_sem, gstage, gin, hstage, hin, step_send, step_recv) = refs
    else:
        terms_ref, back_ref, send_sem, recv_sem = refs
    me = lax.axis_index("dom")
    feat = lax.axis_index("feat")
    greet(n, me, feat, False)
    if inner:
        gstage[...] = grad_ref[...].astype(BF16).reshape(gstage.shape)
    back_ref[me] = terms_ref[me]
    wait_greetings(n - 1)

    def copy_to(target, src, dst, ssem, rsem):
        return pltpu.make_async_remote_copy(
            src_ref=src, dst_ref=dst, send_sem=ssem, recv_sem=rsem,
            device_id={"dom": target}, device_id_type=pl.DeviceIdType.MESH,
        )

    def term_copy(d):
        q = lax.rem(me + d, n)
        return copy_to(q, terms_ref.at[q], back_ref.at[me], send_sem.at[d], recv_sem.at[d])

    def send_terms(first, last):
        def body(k, carry):
            term_copy(mixed(k, n)).start()
            return carry
        lax.fori_loop(first, last, body, 0)

    batch = -(-(n - 1) // 3)

    def each(fn, size):
        def body(d, carry):
            fn(d)
            return carry
        lax.fori_loop(1, size, body, 0)

    if inner:
        outer = n // inner
        z, i = me // inner, lax.rem(me, inner)

        def plane_copy(d, phase, src, dst):
            j = lax.rem(i + d, inner)
            return copy_to(z * inner + j, src(j), dst, step_send.at[phase, d], step_recv.at[phase, d])

        def line_copy(d, phase, src, dst):
            k = lax.rem(z + d, outer)
            return copy_to(k * inner + i, src(k), dst, step_send.at[phase, d], step_recv.at[phase, d])

        def scatter_plane(d):
            return plane_copy(d, 0, lambda j: gstage.at[j], gin.at[i])

        def scatter_line(d):
            return line_copy(d, 1, lambda k: hstage.at[k], hin.at[z])

        def gather_line(d):
            return line_copy(d, 2, lambda k: gall.at[i, z], gall.at[i, z])

        def gather_plane(d):
            return plane_copy(d, 3, lambda j: gall.at[i], gall.at[i])

        each(lambda d: scatter_plane(d).start(), inner)
        send_terms(0, batch)
        gin[i] = gstage[i]
        each(lambda d: scatter_plane(d).wait_recv(), inner)
        hstage[...] = jnp.sum(gin[...].astype(F32), axis=0).astype(BF16)
        each(lambda d: scatter_line(d).start(), outer)
        send_terms(batch, 2 * batch)
        hin[z] = hstage[z]
        each(lambda d: scatter_line(d).wait_recv(), outer)
        gall[i, z] = jnp.sum(hin[...].astype(F32), axis=0).astype(BF16)
        each(lambda d: gather_line(d).start(), outer)
        send_terms(2 * batch, n - 1)
        each(lambda d: gather_line(d).wait_recv(), outer)
        each(lambda d: gather_plane(d).start(), inner)
    else:
        send_terms(0, n - 1)
    each(lambda d: term_copy(d).wait(), n)
    if inner:
        each(lambda d: scatter_plane(d).wait_send(), inner)
        each(lambda d: scatter_line(d).wait_send(), outer)
        each(lambda d: gather_line(d).wait_send(), outer)
        each(lambda d: gather_plane(d).wait(), inner)


def finish_kernel(
    hub_dev, edge, factor, send_ref, hub_ref, feat_ref, direct_ref, back_ref, sum_ref,
    out_ref, self_ref, neigh_ref,
):
    n = back_ref.shape[0]
    half = out_ref.shape[1]
    out_ref[...] = direct_ref[...]

    def add(q, carry):
        rows = pl.ds(pl.multiple_of(send_ref[q] * edge, edge), edge)
        out_ref[rows, :] += back_ref[q, 0:edge, :].astype(F32)
        return carry

    lax.fori_loop(0, n, add, 0)
    hub_total = jnp.sum(back_ref[:, edge:, :].astype(F32), axis=0)
    for h in range(hub_dev):
        row = hub_total[h:h + 1] + hub_total[hub_dev + h:hub_dev + h + 1]
        out_ref[pl.ds(hub_ref[h], 1), :] += row
    total = sum_ref[...].astype(F32) * factor
    swapped = jnp.concatenate([total[:, half:], total[:, :half]], axis=1)
    total = jnp.where(feat_ref[0] == 0, total, swapped)
    self_ref[...] = total[:half]
    neigh_ref[...] = total[half:]


def shards(
    features, self_weight, neighbor_weight, tile_values, tile_row, tile_owner,
    send_tile, tile_count, hub_panel, hub_rows, cotangent,
):
    rows, half = features.shape
    edge = tile_values.shape[1]
    tiles = rows // edge
    n = lax.axis_size("dom")
    hub_dev = hub_rows.shape[0]
    hubs = hub_panel.shape[1]
    wide = 2 * half
    pad = -(-2 * hub_dev // 16) * 16
    tall = edge + pad
    sds = jax.ShapeDtypeStruct
    dma = pltpu.SemaphoreType.DMA
    anywhere = pl.BlockSpec(memory_space=pl.ANY)
    params = functools.partial(pltpu.CompilerParams, vmem_limit_bytes=VMEM_BYTES)

    cols, x_all, c_all, ws_other, wn_other, x_turned = pl.pallas_call(
        functools.partial(exchange_kernel, n, hub_dev),
        out_shape=(
            sds((n, tall, wide), BF16), sds((tiles, edge, wide), BF16), sds((tiles, edge, wide), BF16),
            sds(self_weight.shape, BF16), sds(neighbor_weight.shape, BF16), sds((half, rows), BF16),
        ),
        in_specs=[vmem()] * 4 + [smem()] * 2,
        out_specs=(vmem(),) * 6,
        scratch_shapes=[
            pltpu.VMEM((n, tall, half), BF16),
            dma((n,)), dma((n,)), dma((n,)), dma((n,)), dma((2,)), dma((4,)), dma((4,)),
        ],
        compiler_params=params(collective_id=0, has_side_effects=True),
        name="exchange",
    )(
        features.reshape(tiles, edge, half), cotangent.reshape(tiles, edge, half),
        self_weight, neighbor_weight, send_tile, hub_rows,
    )

    feat_index = lax.axis_index("feat").astype(jnp.int32).reshape(1)
    slots = tile_values.shape[0]
    parts = math.gcd(slots, 4)
    chunks = tiles // math.gcd(tiles, 4)
    layer, grads, direct, terms = pl.pallas_call(
        functools.partial(local_kernel, hub_dev),
        out_shape=(
            sds((tiles, edge, half), BF16), sds((wide, wide), F32),
            sds((tiles, edge, half), F32), sds((n, tall, half), BF16),
        ),
        in_specs=[smem()] * 4 + [vmem(), anywhere, anywhere] + [vmem()] * 4 + [anywhere, vmem(), anywhere],
        out_specs=(anywhere, vmem(), anywhere, vmem()),
        scratch_shapes=[
            pltpu.VMEM((tiles, edge, wide), F32),
            pltpu.VMEM((tiles, edge, edge), F32),
            pltpu.VMEM((tiles, half, edge), BF16),
            pltpu.VMEM((n, half, edge), F32),
            pltpu.VMEM((hubs, half), F32),
            pltpu.VMEM((tiles, edge, wide), BF16),
            pltpu.VMEM((tiles, edge, wide), BF16),
            pltpu.VMEM((half, rows), BF16),
            pltpu.VMEM(tile_values.shape, BF16),
            pltpu.VMEM((tiles, edge, half), BF16),
            pltpu.VMEM((tiles, edge, half), F32),
            pltpu.VMEM((2 * wide, wide), BF16),
            pltpu.VMEM((wide, wide), BF16),
            dma((parts,)), dma((3,)), dma((chunks,)), dma((chunks,)),
        ],
        compiler_params=params(),
        name="local_pass",
    )(
        feat_index, tile_row, tile_owner, tile_count, cols, x_all, c_all,
        self_weight, neighbor_weight, ws_other, wn_other, tile_values, hub_panel.T,
        x_turned,
    )

    factor = 1.0 / math.sqrt(rows * n)
    inner = math.isqrt(n)
    if inner * inner != n or wide % (16 * n):
        inner = 0
    back_shape = sds((n, tall, half), BF16)
    if inner:
        line = (inner, wide // n, wide)
        back, sums = pl.pallas_call(
            functools.partial(return_kernel, n, inner),
            out_shape=(back_shape, sds((inner,) + line, BF16)),
            in_specs=[vmem()] * 2,
            out_specs=(vmem(),) * 2,
            scratch_shapes=[
                dma((n,)), dma((n,)),
                pltpu.VMEM((inner,) + line, BF16), pltpu.VMEM((inner,) + line, BF16),
                pltpu.VMEM(line, BF16), pltpu.VMEM(line, BF16),
                dma((4, inner)), dma((4, inner)),
            ],
            compiler_params=params(collective_id=1, has_side_effects=True),
            name="send_back",
        )(terms, grads)
    else:
        back = pl.pallas_call(
            functools.partial(return_kernel, n, 0),
            out_shape=back_shape,
            in_specs=[vmem()],
            out_specs=vmem(),
            scratch_shapes=[dma((n,)), dma((n,))],
            compiler_params=params(collective_id=1, has_side_effects=True),
            name="send_back",
        )(terms)
        sums = lax.psum(grads, "dom")

    input_grad, self_grad, neighbor_grad = pl.pallas_call(
        functools.partial(finish_kernel, hub_dev, edge, factor),
        out_shape=(sds((rows, half), F32), sds((half, wide), F32), sds((half, wide), F32)),
        in_specs=[smem()] * 3 + [vmem()] * 3,
        out_specs=(vmem(),) * 3,
        compiler_params=params(),
        name="finish",
    )(send_tile, hub_rows, feat_index, direct.reshape(rows, half), back, sums.reshape(wide, wide))
    return layer.reshape(rows, half), self_grad, neighbor_grad, input_grad


def solution(mesh):
    placed = (
        P("dom", "feat"), P("feat", None), P("feat", None), P("dom", None, None), P("dom"), P("dom"),
        P("dom"), P("dom"), P("dom", None), P("dom"), P("dom", "feat"),
    )
    return jax.shard_map(
        shards,
        mesh=mesh,
        in_specs=placed,
        out_specs=(P("dom", "feat"), P("feat", None), P("feat", None), P("dom", "feat")),
        check_vma=False,
    )
```
